256 devices in a mesh: pme: 8 (over z), dom: 32 (over x, y, core).
Axes of the slice: x: 4, y: 4, z: 8, core: 2. Of those that a mesh axis runs over, the one named last changes fastest.
Arguments:
- group_column: int32 [16384, 1], P(('pme', 'dom')), may hold values from 0 to 31, as said below
- group_corner: int32 [3, 16384], P(None, ('pme', 'dom')), may hold values from 0 to 16, as said below
- atom_cell: int32 [3, 524288], P(None, ('pme', 'dom')), may hold values from 0 to 7, as said below
- fraction: float32 [3, 524288], P(None, ('pme', 'dom')), may hold values from 0.25 to 0.75
- charge: float32 [524288], P(('pme', 'dom')), may hold values from -4 to 4
- cluster_pairs: int32 [2, 262144], P(None, ('pme', 'dom')), may hold values from 0 to 263, as said below
Outputs:
- forces: float32 [3, 524288], P(None, ('pme', 'dom'))
The draws below stay inside these ranges and needn't reach their ends.
Inputs may be any that keep to these rules, and one draw needn't show every extreme that they name: `group_column`: in each aligned block of 64 rows (the groups of one device) no column is named by more than 4 rows, and in every block one column is named by exactly 4. `group_corner`: row 0 lies in 0 to 16, row 1 in 0 to 16, row 2 in 0 to 0. `atom_cell`: row 0 is below 8, row 1 below 8, row 2 below 4; within each group of 32 consecutive atoms the three rows form distinct triples. `cluster_pairs`: row 0 names one of the 256 clusters of the device that holds the column. Row 1 names either another cluster of the same block of 4 clusters (clusters 4 * k to 4 * k + 3) of that device, or 256 + c with c below 8, cluster c of the next device along dom.
All inputs are finite; a program needn't handle non-finite values.
Results may differ from the reference program's by a relative error of at most 0.0003.
Values sent between devices are 32-bit elements; how exact they have to be, the bound alone decides.
No kernel may reach another device: no remote copies, remote signals or barrier semaphores. Data moves between devices by JAX's collectives and lax.ppermute only.
A program may use at most 128 MiB of HBM per device.

```python
import math
import jax
import jax.numpy as jnp
from jax import lax

NX = 768
NY = 768
NZ = 32
ATOMS_GROUP = 32
CLUSTER = 8
GBX = 8
GROUPS_DEV = 64
CLUST_DEV = 256
GROUP_CLUSTERS = 4
PAIRS_DEV = 1024
GROUPS = 16384
ATOMS = 524288
PAIRS = 262144
CAPG = 4
HALO_GROUPS = 2
HALO_PAIRS = 32
XD = 24
YP = 24
ZP = 4
GBY = 8
GBZ = 4
N_PME = 8
N_DOM = 32
DEVICES = 256


def shared_layout(key):
    key = jax.random.fold_in(key, 5)
    key_col, key_y, key_z = jax.random.split(key, 3)
    row_column = jax.random.randint(key_col, (N_PME,), 0, N_DOM)
    rim_y = jax.random.randint(key_y, (N_PME, HALO_GROUPS), 0, YP - GBY + 1)
    rim_z = jax.random.randint(key_z, (N_PME, HALO_GROUPS), 0, ZP - GBZ + 1)
    return (row_column, rim_y, rim_z)


def draw_group_column(key, part):
    row_column, rim_y, rim_z = shared_layout(key)
    key = jax.random.fold_in(key, 7)
    block_keys = jax.random.split(key, DEVICES)
    others = GROUPS_DEV - 2 * HALO_GROUPS

    def pick_slots(block_key):
        return jax.random.permutation(block_key, (N_DOM - 1) * CAPG)[:others] // CAPG
    picks = jax.vmap(pick_slots)(block_keys)
    own = row_column[jnp.arange(DEVICES) // N_DOM][:, None]
    middle = picks + (picks >= own).astype(jnp.int32)
    rims = jnp.broadcast_to(own, (DEVICES, HALO_GROUPS))
    block = jnp.concatenate([rims, middle, rims], axis=1)
    return block.reshape(GROUPS, 1).astype(jnp.int32)


def draw_group_corner(key, part):
    row_column, rim_y, rim_z = shared_layout(key)
    key = jax.random.fold_in(key, 11)
    key_x, key_y, key_z = jax.random.split(key, 3)
    corner_x = jax.random.randint(key_x, (DEVICES, GROUPS_DEV), 0, XD - GBX + 1)
    corner_y = jax.random.randint(key_y, (DEVICES, GROUPS_DEV), 0, YP - GBY + 1)
    corner_z = jax.random.randint(key_z, (DEVICES, GROUPS_DEV), 0, ZP - GBZ + 1)
    serial = jnp.arange(GROUPS_DEV)
    first = serial < HALO_GROUPS
    last = serial >= GROUPS_DEV - HALO_GROUPS
    rim_index = jnp.clip(jnp.where(first, serial, serial - (GROUPS_DEV - HALO_GROUPS)), 0, HALO_GROUPS - 1)
    pme_rows = jnp.arange(DEVICES) // N_DOM
    rim_y_full = rim_y[pme_rows][:, rim_index]
    rim_z_full = rim_z[pme_rows][:, rim_index]
    either = jnp.logical_or(first, last)[None, :]
    corner_x = jnp.where(first[None, :], 0, jnp.where(last[None, :], XD - GBX, corner_x))
    corner_y = jnp.where(either, rim_y_full, corner_y)
    corner_z = jnp.where(either, rim_z_full, corner_z)
    return jnp.stack([corner_x.reshape(GROUPS), corner_y.reshape(GROUPS), corner_z.reshape(GROUPS)]).astype(jnp.int32)


def draw_atom_cell(key, part):
    key = jax.random.fold_in(key, 23)
    group_keys = jax.random.split(key, GROUPS)

    def pick_cells(group_key):
        return jax.random.permutation(group_key, GBX * GBY * GBZ)[:ATOMS_GROUP]
    picks = jax.vmap(pick_cells)(group_keys)
    cell_x = picks % GBX
    cell_y = picks // GBX % GBY
    cell_z = picks // (GBX * GBY)
    return jnp.stack([cell_x, cell_y, cell_z]).reshape(3, ATOMS).astype(jnp.int32)


def draw_cluster_pairs(key, part):
    key = jax.random.fold_in(key, 37)
    key_first, key_step, key_rim, key_left, key_right = jax.random.split(key, 5)
    inner = PAIRS_DEV - HALO_PAIRS
    first = jax.random.randint(key_first, (DEVICES, inner), 0, CLUST_DEV)
    stride = jax.random.randint(key_step, (DEVICES, inner), 1, GROUP_CLUSTERS)
    second = first // GROUP_CLUSTERS * GROUP_CLUSTERS + (first % GROUP_CLUSTERS + stride) % GROUP_CLUSTERS
    rim = jax.random.randint(key_rim, (DEVICES, HALO_PAIRS), 0, HALO_GROUPS)
    left_pick = jax.random.randint(key_left, (DEVICES, HALO_PAIRS), 0, GROUP_CLUSTERS)
    right_pick = jax.random.randint(key_right, (DEVICES, HALO_PAIRS), 0, GROUP_CLUSTERS)
    rim = rim.at[:, 0].set(HALO_GROUPS - 1)
    right_pick = right_pick.at[:, 0].set(GROUP_CLUSTERS - 1)
    rim_first = (GROUPS_DEV - HALO_GROUPS + rim) * GROUP_CLUSTERS + left_pick
    rim_second = CLUST_DEV + rim * GROUP_CLUSTERS + right_pick
    row_first = jnp.concatenate([rim_first, first], axis=1).reshape(PAIRS)
    row_second = jnp.concatenate([rim_second, second], axis=1).reshape(PAIRS)
    return jnp.stack([row_first, row_second]).astype(jnp.int32)


def level_of(own_key, shape, shards, least, top_value):
    loudness = 1.0
    for dim, parts in shards:
        draws = jax.random.uniform(jax.random.fold_in(jax.random.fold_in(own_key, 6), dim), (parts,), jnp.float32, least / len(shards), top_value / len(shards))
        loudness = loudness * jnp.repeat(jnp.exp(draws), shape[dim] // parts).reshape((-1,) + (1,) * (len(shape) - 1 - dim))
    return loudness


def noise(own_key, dims, width, limit, shards=(), kind=jnp.bfloat16):
    entries = jax.random.normal(own_key, dims, jnp.float32) * width
    if len(shards) > 0:
        entries = level_of(own_key, dims, shards, -0.22, 0.18) * entries
    return jnp.clip(entries, min=-limit, max=limit).astype(kind)


def setup_inputs(seed: int = 0) -> dict:
    splits = jax.random.split(jax.random.key(seed), 7)
    return {
        "group_column": draw_group_column(jax.random.fold_in(splits[6], 71), 0),
        "group_corner": draw_group_corner(jax.random.fold_in(splits[6], 71), 0),
        "atom_cell": draw_atom_cell(jax.random.fold_in(splits[6], 71), 0),
        "fraction": jnp.clip(0.25 + 0.5 * jax.random.uniform(splits[3], (3, ATOMS), jnp.float32) ** level_of(splits[3], (3, ATOMS), ((1, 256),), -0.2, 0.2), 0.25, 0.75),
        "charge": noise(splits[4], (ATOMS,), 1.0, 4.0, ((0, 256),), jnp.float32),
        "cluster_pairs": draw_cluster_pairs(jax.random.fold_in(splits[6], 71), 0),
    }


BETA = 0.35
HIGHEST = lax.Precision.HIGHEST

def spline_weights(weight):
    remain = 1.0 - weight
    squared = weight * weight
    cubed = squared * weight
    spline = jnp.stack([remain * remain * remain / 6.0, (3.0 * cubed - 6.0 * squared + 4.0) / 6.0, (-3.0 * cubed + 3.0 * squared + 3.0 * weight + 1.0) / 6.0, cubed / 6.0])
    slopes = jnp.stack([-0.5 * remain * remain, 0.5 * (3.0 * squared - 4.0 * weight), 0.5 * (-3.0 * squared + 2.0 * weight + 1.0), 0.5 * squared])
    return (spline, slopes)

def folded_frequency(wavenum, length):
    signed = jnp.where(2 * wavenum < length, wavenum, wavenum - length)
    return signed.astype(jnp.float32) / length

def spline_modulus(wavenum, length):
    cosine = jnp.cos(2.0 * math.pi / length * wavenum.astype(jnp.float32))
    factor = 2.0 / 3.0 + cosine / 3.0
    return 1.0 / (factor * factor)

def influence_values(wave_x, wave_y, wave_z):
    along_x = folded_frequency(wave_x, NX)
    along_y = folded_frequency(wave_y, NY)
    along_z = folded_frequency(wave_z, NZ)
    squared = along_x * along_x + along_y * along_y + along_z * along_z
    nonzero = jnp.where(squared > 0.0, squared, 1.0)
    kernel = jnp.exp(-(math.pi / BETA) * (math.pi / BETA) * squared)
    kernel = kernel * spline_modulus(wave_x, NX) * spline_modulus(wave_y, NY) * spline_modulus(wave_z, NZ)
    kernel = kernel / (math.pi * nonzero)
    return jnp.where(squared > 0.0, kernel, 0.0)

def reference(group_column, group_corner, atom_cell, fraction, charge, cluster_pairs):
    groups = group_column.shape[0]
    serial = jnp.arange(groups, dtype=jnp.int32)
    device = serial // GROUPS_DEV
    pme_row = device // N_DOM
    dom_col = device % N_DOM
    column = group_column[:, 0]
    offsets = jnp.stack([dom_col * XD, column * YP, pme_row * ZP])
    base_cell = jnp.repeat(group_corner + offsets, ATOMS_GROUP, axis=1) + atom_cell
    position = base_cell.astype(jnp.float32) + fraction
    floor_part = jnp.floor(position)
    weight = position - floor_part
    cell_index = floor_part.astype(jnp.int32)
    spline, slopes = spline_weights(weight)
    stencil_steps = jnp.arange(4, dtype=jnp.int32)
    x_sites = (cell_index[0][None, :] + stencil_steps[:, None]) % NX
    y_sites = (cell_index[1][None, :] + stencil_steps[:, None]) % NY
    z_sites = (cell_index[2][None, :] + stencil_steps[:, None]) % NZ
    flat_index = (x_sites[:, None, None, :] * NY + y_sites[None, :, None, :]) * NZ + z_sites[None, None, :, :]
    values = charge[None, None, None, :] * spline[:, 0][:, None, None, :] * spline[:, 1][None, :, None, :] * spline[:, 2][None, None, :, :]
    charge_grid = jnp.zeros((NX * NY * NZ,), jnp.float32).at[flat_index.reshape(-1)].add(values.reshape(-1))
    charge_grid = charge_grid.reshape(NX, NY, NZ)
    waves_x = jnp.arange(NX, dtype=jnp.int32)
    waves_y = jnp.arange(NY, dtype=jnp.int32)
    waves_z = jnp.arange(NZ, dtype=jnp.int32)
    kernel = influence_values(waves_x[:, None, None], waves_y[None, :, None], waves_z[None, None, :])
    potential = jnp.real(jnp.fft.ifftn(jnp.fft.fftn(charge_grid) * kernel))
    sampled = potential.reshape(-1)[flat_index]
    grad_x = jnp.einsum('ijka,ia,ja,ka->a', sampled, slopes[:, 0], spline[:, 1], spline[:, 2], precision=HIGHEST)
    grad_y = jnp.einsum('ijka,ia,ja,ka->a', sampled, spline[:, 0], slopes[:, 1], spline[:, 2], precision=HIGHEST)
    grad_z = jnp.einsum('ijka,ia,ja,ka->a', sampled, spline[:, 0], spline[:, 1], slopes[:, 2], precision=HIGHEST)
    pme_force = -charge[None, :] * jnp.stack([grad_x, grad_y, grad_z])
    pair_count = cluster_pairs.shape[1]
    pair_owner = jnp.arange(pair_count, dtype=jnp.int32) // PAIRS_DEV
    next_owner = pair_owner // N_DOM * N_DOM + (pair_owner % N_DOM + 1) % N_DOM
    second = cluster_pairs[1]
    beyond = second >= CLUST_DEV
    left_id = cluster_pairs[0] + pair_owner * CLUST_DEV
    right_id = jnp.where(beyond, next_owner * CLUST_DEV + second - CLUST_DEV, pair_owner * CLUST_DEV + second)
    lifted = jnp.logical_and(beyond, pair_owner % N_DOM == N_DOM - 1)
    lift = lifted.astype(jnp.float32) * NX
    clusters = position.shape[1] // CLUSTER
    coords = position.reshape(3, clusters, CLUSTER)
    charges = charge.reshape(clusters, CLUSTER)
    left_pos = coords[:, left_id, :]
    right_pos = coords[:, right_id, :]
    zero_lift = jnp.zeros_like(lift)
    right_pos = right_pos + jnp.stack([lift, zero_lift, zero_lift])[:, :, None]
    offset_vec = left_pos[:, :, :, None] - right_pos[:, :, None, :]
    dist_sq = lax.optimization_barrier(jnp.sum(offset_vec * offset_vec, axis=0))
    distance = jnp.sqrt(dist_sq)
    strength = charges[left_id][:, :, None] * charges[right_id][:, None, :]
    strength = strength * (lax.erfc(BETA * distance) / distance + 2.0 * BETA / math.sqrt(math.pi) * jnp.exp(-(BETA * BETA) * dist_sq)) / dist_sq
    pair_force = strength[None] * offset_vec
    on_left = lax.optimization_barrier(jnp.sum(pair_force, axis=3))
    on_right = lax.optimization_barrier(jnp.sum(pair_force, axis=2))
    summed = jnp.zeros((3, clusters, CLUSTER), jnp.float32)
    summed = summed.at[:, left_id, :].add(on_left).at[:, right_id, :].add(-on_right)
    nonbonded_force = summed.reshape(3, clusters * CLUSTER)
    return pme_force + nonbonded_force
```

```python
import math

import jax
import jax.numpy as jnp
import ml_dtypes
import numpy as np
from jax import lax
from jax.experimental import pallas as pl
from jax.experimental.pallas import tpu as pltpu
from jax.sharding import PartitionSpec as P

NX = 768
NY = 768
NZ = 32
N_DOM = 32
N_PME = 8
DEVICES = 256
XD = 24
YP = 24
ZP = 4
GROUPS = 64
ATOMS = 2048
PAIRS = 1024
CLUSTERS = 256
HALO_CLUSTERS = 8
HALO_ATOMS = 64
XW = 32
MODES = 3
BLOCKS = 98
BETA = 0.35
VMEM_LIMIT = 24 * 1024 * 1024

F32 = jnp.float32
BF16 = jnp.bfloat16

ERFC_Q = (
    0.2820947951,
    0.2820937768,
    0.2468838798,
    0.1753240754,
    0.0934147485,
    -0.05905091002,
    0.1318500403,
    -0.4545637183,
    0.493385742,
    -0.2346054907,
    0.04317306594,
)


def real_basis(length):
    point = np.arange(length)
    rows = np.zeros((length, length))
    waves = np.zeros(length, np.int64)
    rows[0] = 1.0 / math.sqrt(length)
    for k in range(1, length // 2):
        angle = 2.0 * math.pi * (k * point % length) / length
        rows[2 * k - 1] = math.sqrt(2.0 / length) * np.cos(angle)
        rows[2 * k] = math.sqrt(2.0 / length) * np.sin(angle)
        waves[2 * k - 1] = k
        waves[2 * k] = k
    rows[length - 1] = (1.0 - 2.0 * (point % 2)) / math.sqrt(length)
    waves[length - 1] = length // 2
    return rows, waves


def wave_factors(waves, length):
    freq = waves / length
    modulus = 1.0 / (2.0 / 3.0 + np.cos(2.0 * math.pi * waves / length) / 3.0) ** 2
    return freq * freq, np.exp(-((math.pi / BETA) ** 2) * freq * freq) * modulus


def halves(table):
    table = table.astype(np.float32)
    high = table.astype(ml_dtypes.bfloat16)
    low = (table - high.astype(np.float32)).astype(ml_dtypes.bfloat16)
    return high, low


def split(value):
    high = value.astype(BF16)
    low = (value - high.astype(F32)).astype(BF16)
    return high, low


def dot(a, b):
    return jnp.dot(a, b, preferred_element_type=F32)


def dot_nt(a, b):
    return lax.dot_general(a, b, (((1,), (1,)), ((), ())), preferred_element_type=F32)


def dot_tn(a, b):
    return lax.dot_general(a, b, (((0,), (0,)), ((), ())), preferred_element_type=F32)


def iota(shape, dim):
    return lax.broadcasted_iota(jnp.int32, shape, dim)


def spline(u):
    d = jnp.abs(u)
    a = jnp.maximum(2.0 - d, 0.0)
    b = jnp.maximum(1.0 - d, 0.0)
    return (a * a * a - 4.0 * (b * b * b)) * (1.0 / 6.0)


def spline_slope(u):
    d = jnp.abs(u)
    a = jnp.maximum(2.0 - d, 0.0)
    b = jnp.maximum(1.0 - d, 0.0)
    slope = 0.5 * (a * a) - 2.0 * (b * b)
    return slope, (a * a * a - 4.0 * (b * b * b)) * (1.0 / 6.0)


def weights_of(u):
    slope, value = spline_slope(u)
    return value, jnp.where(u < 0.0, -slope, slope)


def prepare_kernel(place, col, corner, cell, fraction, charge, atoms, edge):
    group = iota((GROUPS, ATOMS), 0)
    hot = jnp.where((iota((GROUPS, ATOMS), 1) >> 5) == group, 1.0, 0.0).astype(BF16)
    rep_corner = dot(corner[...].astype(F32).astype(BF16), hot)
    rep_col = dot(
        jnp.broadcast_to(col[...].astype(F32), (8, GROUPS)).astype(BF16), hot
    )[0:1]
    base = rep_corner + cell[...].astype(F32)
    first = (place[0] * XD).astype(F32)
    third = (place[1] * ZP).astype(F32)
    along_x = (base[0:1] + first) + fraction[0:1, :]
    along_y = (base[1:2] + rep_col * float(YP)) + fraction[1:2, :]
    along_z = (base[2:3] + third) + fraction[2:3, :]
    atoms[...] = jnp.zeros((8, ATOMS), F32)
    atoms[0:1, :] = along_x
    atoms[1:2, :] = along_y
    atoms[2:3, :] = along_z
    atoms[3:4, :] = charge[...]
    lowest = (col[...] * YP + corner[1:2, :]).astype(F32)
    atoms[4:5, 0:GROUPS] = lowest
    edge[...] = atoms[:, 0:128]


def y_blocks(ya, batch, lane):
    starts = [ya[4 * batch + j] for j in range(4)]
    row = jnp.where(
        lane < 64,
        jnp.where(lane < 32, starts[0], starts[1]),
        jnp.where(lane < 96, starts[2], starts[3]),
    )
    return starts, (row * 8).astype(F32)


def masked_blocks(weights, lane):
    return jnp.concatenate(
        [jnp.where((lane >> 5) == j, weights, 0.0) for j in range(4)], axis=0
    )


def spread_batches(origin_x, origin_z, ya, atoms, grid):
    lane = iota((1, 128), 1)
    step_x = iota((XW, 128), 0).astype(F32)
    step_y = iota((24, 128), 0).astype(F32)
    step_z = iota((8, 128), 0).astype(F32)
    for batch in range(ATOMS // 128):
        own = slice(128 * batch, 128 * batch + 128)
        starts, base_y = y_blocks(ya, batch, lane)
        xs = (atoms[0:1, own] - origin_x) + 1.0
        ys = (atoms[1:2, own] - base_y) + 1.0
        zs = (atoms[2:3, own] - origin_z) + 1.0
        wx = spline(step_x - xs)
        wz = spline(step_z - zs) * atoms[3:4, own]
        wy = masked_blocks(spline(step_y - ys), lane)
        charged = jnp.concatenate([wx * wz[z : z + 1] for z in range(ZP)], axis=0)
        c_high, c_low = split(charged)
        y_high, y_low = split(wy)
        added = dot_nt(y_high, c_high) + (dot_nt(y_high, c_low) + dot_nt(y_low, c_high))
        for j in range(4):
            part = added[24 * j : 24 * j + 24].reshape(3, 8, 128)
            grid[pl.ds(starts[j], 3)] = grid[pl.ds(starts[j], 3)] + part


def spread_own_kernel(place, ya, atoms, grid):
    grid[...] = jnp.zeros((BLOCKS, 8, 128), F32)
    origin_x = (place[0] * XD).astype(F32)
    origin_z = (place[1] * ZP).astype(F32)
    spread_batches(origin_x, origin_z, ya, atoms, grid)


def neighbour_origin(place):
    behind = (place[1] + (N_PME - 1)) & (N_PME - 1)
    return (place[0] * XD).astype(F32), (behind * ZP + ZP).astype(F32)


def spread_rest_kernel(place, ya, atoms, own, table_high, table_low, out, grid):
    grid[...] = own[...]
    origin_x, origin_z = neighbour_origin(place)
    spread_batches(origin_x, origin_z, ya, atoms, grid)
    grid[0:2] = grid[0:2] + grid[96:98]
    g_high, g_low = split(grid[0:96].reshape(NY, 128))
    both = dot(table_high[...], jnp.concatenate([g_high, g_low], axis=1))
    out[...] = both[:, :128] + (both[:, 128:] + dot(table_low[...], g_high))


def filter_kernel(
    place, y_square, y_factor, held, fx_high, fx_low, kz_high, kz_low, tz_high, tz_low,
    x_square, x_factor, z_square, z_factor, out, work,
):
    lane = iota((8, 128), 1) >> 5
    for m in range(MODES):
        for a in range(8):
            blocks = [held[pl.ds((4 * a + b) * 24 + m, 8, stride=3), :] for b in range(4)]
            for z in range(ZP):
                tile = None
                for b in range(4):
                    shift = (32 * (b - z)) % 128
                    moved = blocks[b] if shift == 0 else pltpu.roll(blocks[b], shift, 1)
                    tile = moved if tile is None else jnp.where(lane == b, moved, tile)
                row = m * NZ + z * 8
                work[row : row + 8, 128 * a : 128 * a + 128] = tile
    x_high, x_low = split(work[...])
    waves = dot(x_high, fx_high[...]) + (dot(x_low, fx_high[...]) + dot(x_high, fx_low[...]))
    w_high, w_low = split(waves)
    full = dot(kz_high[...], w_high) + (dot(kz_high[...], w_low) + dot(kz_low[...], w_high))
    device = place[0] * N_PME + place[1]
    scaled = []
    for m in range(MODES):
        mode = device * MODES + m
        square = (x_square[...] + z_square[:, 0:1]) + y_square[mode]
        factor = (x_factor[...] * z_factor[:, 0:1]) * y_factor[mode]
        nonzero = jnp.where(square > 0.0, square, 1.0)
        influence = jnp.where(square > 0.0, factor / nonzero, 0.0)
        scaled.append(full[m * NZ : m * NZ + NZ] * influence)
    s_high, s_low = split(jnp.concatenate(scaled, axis=0))
    back = dot(tz_high[...], s_high) + (dot(tz_high[...], s_low) + dot(tz_low[...], s_high))
    b_high, b_low = split(back)
    work[...] = dot_nt(b_high, fx_high[...]) + (
        dot_nt(b_low, fx_high[...]) + dot_nt(b_high, fx_low[...])
    )
    for m in range(MODES):
        for a in range(8):
            tiles = [
                work[m * NZ + z * 8 : m * NZ + z * 8 + 8, 128 * a : 128 * a + 128]
                for z in range(ZP)
            ]
            for b in range(4):
                block = None
                for z in range(ZP):
                    shift = (32 * (z - b)) % 128
                    moved = tiles[z] if shift == 0 else pltpu.roll(tiles[z], shift, 1)
                    block = moved if block is None else jnp.where(lane == z, moved, block)
                out[pl.ds((4 * a + b) * 24 + m, 8, stride=3), :] = block


def gather_batches(origin_x, origin_z, ya, atoms, grid, store):
    lane = iota((1, 128), 1)
    step_x = iota((XW, 128), 0).astype(F32)
    step_y = iota((24, 128), 0).astype(F32)
    step_z = iota((8, 128), 0).astype(F32)
    for batch in range(ATOMS // 128):
        own = slice(128 * batch, 128 * batch + 128)
        starts, base_y = y_blocks(ya, batch, lane)
        xs = (atoms[0:1, own] - origin_x) + 1.0
        ys = (atoms[1:2, own] - base_y) + 1.0
        zs = (atoms[2:3, own] - origin_z) + 1.0
        wx, sx = weights_of(step_x - xs)
        wy, sy = weights_of(step_y - ys)
        wz, sz = weights_of(step_z - zs)
        block = jnp.concatenate(
            [grid[pl.ds(starts[j], 3)].reshape(24, 128) for j in range(4)], axis=0
        )
        b_high, b_low = split(block)
        y_both = jnp.concatenate([masked_blocks(wy, lane), masked_blocks(sy, lane)], axis=1)
        y_high, y_low = split(y_both)
        sampled = dot_tn(b_high, y_high) + (dot_tn(b_low, y_high) + dot_tn(b_high, y_low))
        along_x = along_y = along_z = jnp.zeros((XW, 128), F32)
        for z in range(ZP):
            value = sampled[XW * z : XW * z + XW, :128]
            slope = sampled[XW * z : XW * z + XW, 128:]
            along_x = along_x + value * wz[z : z + 1]
            along_y = along_y + slope * wz[z : z + 1]
            along_z = along_z + value * sz[z : z + 1]
        minus = -atoms[3:4, own]
        store(
            own,
            minus * jnp.sum(along_x * sx, axis=0, keepdims=True),
            minus * jnp.sum(along_y * wx, axis=0, keepdims=True),
            minus * jnp.sum(along_z * wx, axis=0, keepdims=True),
        )


def gather_rest_kernel(place, ya, atoms, held, table_high, table_low, grid, out):
    h_high, h_low = split(held[...])
    both = dot(table_high[...], jnp.concatenate([h_high, h_low], axis=1))
    potential = both[:, :128] + (both[:, 128:] + dot(table_low[...], h_high))
    grid[0:96] = potential.reshape(96, 8, 128)
    grid[96:98] = potential[0:16].reshape(2, 8, 128)
    origin_x, origin_z = neighbour_origin(place)

    def store(own, fx, fy, fz):
        out[0:1, own] = fx
        out[1:2, own] = fy
        out[2:3, own] = fz

    gather_batches(origin_x, origin_z, ya, atoms, grid, store)


def gather_own_kernel(place, ya, atoms, grid, near, halo, out):
    origin_x = (place[0] * XD).astype(F32)
    origin_z = (place[1] * ZP).astype(F32)

    def store(own, fx, fy, fz):
        forces = [fx, fy, fz]
        for f in range(3):
            total = forces[f] + near[f : f + 1, own]
            if own.start == 0:
                total = total + halo[f : f + 1, :]
            out[f : f + 1, own] = total

    gather_batches(origin_x, origin_z, ya, atoms, grid, store)


def pair_strength(dist_sq):
    inverse = lax.rsqrt(dist_sq)
    inverse = inverse * (1.5 - 0.5 * dist_sq * inverse * inverse)
    scaled = BETA * (dist_sq * inverse)
    t = 1.0 / (1.0 + 0.5 * scaled)
    poly = jnp.full_like(t, ERFC_Q[-1])
    for coefficient in ERFC_Q[-2::-1]:
        poly = poly * t + coefficient
    fall = jnp.exp(-(BETA * BETA) * dist_sq)
    bracket = t * poly * inverse + 2.0 * BETA / math.sqrt(math.pi)
    return fall * bracket * (inverse * inverse)


def nonbonded_kernel(place, atoms, turned, pairs, beyond, near, halo, weight, repeated, columns):
    left = pairs[0:1, :]
    right = pairs[1:2, :]
    inside = right < CLUSTERS
    cluster = iota((CLUSTERS, PAIRS), 0)
    hot_left = jnp.where(cluster == left, 1.0, 0.0).astype(BF16)
    hot_right = jnp.where(cluster == right, 1.0, 0.0).astype(BF16)
    code = iota((16, PAIRS), 0)
    code_left = jnp.where(
        code == jnp.where(inside, right & 3, right - (CLUSTERS - 4)), 1.0, 0.0
    ).astype(BF16)
    code_right = jnp.where(
        code == jnp.where(inside, left & 3, -1), 1.0, 0.0
    ).astype(BF16)
    count = dot_nt(code_left, hot_left) + dot_nt(code_right, hot_right)
    n_high, n_low = split(count)
    expand = jnp.where(
        (iota((CLUSTERS, ATOMS), 1) >> 3) == iota((CLUSTERS, ATOMS), 0), 1.0, 0.0
    ).astype(BF16)
    weight[...] = dot(n_high, expand) + dot(n_low, expand)
    turn_1 = turned[...].astype(BF16)
    rest = turned[...] - turn_1.astype(F32)
    turn_2 = rest.astype(BF16)
    turn_3 = (rest - turn_2.astype(F32)).astype(BF16)
    spreading = jnp.where(
        (iota((GROUPS, ATOMS), 1) >> 5) == iota((GROUPS, ATOMS), 0), 1.0, 0.0
    ).astype(BF16)
    repeated[...] = (dot(turn_1, spreading) + dot(turn_2, spreading)) + dot(turn_3, spreading)
    row = iota((8, 128), 0)
    lane = iota((8, 128), 1)
    for tile in range(ATOMS // 128):
        own = slice(128 * tile, 128 * tile + 128)
        px, py, pz = atoms[0:1, own], atoms[1:2, own], atoms[2:3, own]
        sum_x = sum_y = sum_z = jnp.zeros((8, 128), F32)
        for i in range(4):
            dx = px - repeated[8 * i : 8 * i + 8, own]
            dy = py - repeated[32 + 8 * i : 40 + 8 * i, own]
            dz = pz - repeated[64 + 8 * i : 72 + 8 * i, own]
            other = repeated[96 + 8 * i : 104 + 8 * i, own]
            dist_sq = (dx * dx + dy * dy) + dz * dz
            itself = (lane & 31) == (row + 8 * i)
            dist_sq = jnp.where(itself, 1.0, dist_sq)
            strength = pair_strength(dist_sq) * (other * weight[i : i + 1, own])
            sum_x = sum_x + strength * dx
            sum_y = sum_y + strength * dy
            sum_z = sum_z + strength * dz
        near[0:1, own] = jnp.sum(sum_x, axis=0, keepdims=True)
        near[1:2, own] = jnp.sum(sum_y, axis=0, keepdims=True)
        near[2:3, own] = jnp.sum(sum_z, axis=0, keepdims=True)
    lift = jnp.where(place[0] == N_DOM - 1, float(NX), 0.0)
    upright = jnp.transpose(jnp.concatenate([beyond[...]] * 16, axis=0))
    columns[...] = jnp.zeros((128, 128), F32)
    for c in range(HALO_CLUSTERS):
        part = upright[8 * c : 8 * c + 8]
        hx = part[:, 0:1] + lift
        hy = part[:, 1:2]
        hz = part[:, 2:3]
        hq = part[:, 3:4]
        sum_x = sum_y = sum_z = jnp.zeros((8, 128), F32)
        for tile in range(ATOMS // 128):
            own = slice(128 * tile, 128 * tile + 128)
            dx = atoms[0:1, own] - hx
            dy = atoms[1:2, own] - hy
            dz = atoms[2:3, own] - hz
            dist_sq = (dx * dx + dy * dy) + dz * dz
            both = weight[4 + c : 5 + c, own]
            strength = pair_strength(dist_sq) * both
            on_own = strength * hq
            near[0:1, own] = near[0:1, own] + jnp.sum(on_own * dx, axis=0, keepdims=True)
            near[1:2, own] = near[1:2, own] + jnp.sum(on_own * dy, axis=0, keepdims=True)
            near[2:3, own] = near[2:3, own] + jnp.sum(on_own * dz, axis=0, keepdims=True)
            on_halo = strength * atoms[3:4, own]
            sum_x = sum_x - on_halo * dx
            sum_y = sum_y - on_halo * dy
            sum_z = sum_z - on_halo * dz
        force_x = jnp.sum(sum_x, axis=1, keepdims=True) * hq
        force_y = jnp.sum(sum_y, axis=1, keepdims=True) * hq
        force_z = jnp.sum(sum_z, axis=1, keepdims=True) * hq
        columns[8 * c : 8 * c + 8, :] = jnp.where(
            lane == 0, force_x, jnp.where(lane == 1, force_y, jnp.where(lane == 2, force_z, 0.0))
        )
    halo[...] = jnp.transpose(columns[...])[0:8]
    for f in range(3):
        near[f : f + 1, :] = near[f : f + 1, :] * atoms[3:4, :]


def call(kernel, outs, ins, scratch=(), flops=1_000_000):
    vmem = pl.BlockSpec(memory_space=pltpu.VMEM)
    smem = pl.BlockSpec(memory_space=pltpu.SMEM)
    in_specs = [smem if kind == "s" else vmem for kind, _ in ins]
    many = isinstance(outs, list)
    return pl.pallas_call(
        kernel,
        out_shape=outs,
        in_specs=in_specs,
        out_specs=[vmem] * len(outs) if many else vmem,
        scratch_shapes=list(scratch),
        compiler_params=pltpu.CompilerParams(vmem_limit_bytes=VMEM_LIMIT),
        cost_estimate=pl.CostEstimate(flops=flops, bytes_accessed=1_000_000, transcendentals=0),
    )(*[x for _, x in ins])


def shape(*dims):
    return jax.ShapeDtypeStruct(dims, F32)


def permuted(x, axis, by):
    length = lax.axis_size(axis)
    return lax.ppermute(x, axis, [(i, (i + by) % length) for i in range(length)])


def exchange(x):
    sent = x.reshape(DEVICES, 1, MODES * 128)
    return lax.all_to_all(sent, ("dom", "pme"), 0, 0).reshape(DEVICES * MODES, 128)


def tables():
    along_y, y_waves = real_basis(NY)
    along_x, x_waves = real_basis(NX)
    along_z, z_waves = real_basis(NZ)
    folded = np.zeros((N_DOM * XW, NX))
    for q in range(N_DOM):
        for x in range(XD + 3):
            folded[q * XW + x] = along_x[:, (q * XD + x) % NX]
    order = np.array([4 * p + z for z in range(ZP) for p in range(N_PME)])
    z_rows = np.kron(np.eye(MODES), along_z[:, order])
    y_square, y_factor = wave_factors(y_waves, NY)
    x_square, x_factor = wave_factors(x_waves, NX)
    z_square, z_factor = wave_factors(z_waves, NZ)
    f32 = np.float32
    return {
        "y": halves(along_y),
        "y_back": halves(along_y.T),
        "x": halves(folded),
        "z": halves(z_rows),
        "z_back": halves(z_rows.T),
        "y_square": y_square.astype(f32),
        "y_factor": y_factor.astype(f32),
        "x_square": x_square.astype(f32)[None, :],
        "x_factor": (x_factor / math.pi).astype(f32)[None, :],
        "z_square": np.repeat(z_square.astype(f32)[:, None], 128, axis=1),
        "z_factor": np.repeat(z_factor.astype(f32)[:, None], 128, axis=1),
    }


def make_shards(table):
    def shards(group_column, group_corner, atom_cell, fraction, charge, cluster_pairs):
        slot = jnp.arange(8, dtype=jnp.int32)
        place = jnp.where(slot == 0, lax.axis_index("dom"), lax.axis_index("pme"))
        place = place.astype(jnp.int32)
        column = group_column.reshape(1, GROUPS)
        atoms, edge = call(
            prepare_kernel,
            [shape(8, ATOMS), shape(8, 128)],
            [
                ("s", place), ("v", column), ("v", group_corner), ("v", atom_cell),
                ("v", fraction), ("v", charge.reshape(1, ATOMS)),
            ],
        )
        behind = permuted(atoms, "pme", 1)
        beyond = permuted(edge, "dom", -1)
        ya = (column[0] * YP + group_corner[1]) >> 3
        own_grid = call(
            spread_own_kernel,
            shape(BLOCKS, 8, 128),
            [("s", place), ("s", ya), ("v", atoms)],
            flops=3_000_000_000,
        )
        ya_behind = behind[4, :GROUPS].astype(jnp.int32) >> 3
        spectrum = call(
            spread_rest_kernel,
            shape(NY, 128),
            [
                ("s", place), ("s", ya_behind), ("v", behind), ("v", own_grid),
                ("v", table["y"][0]), ("v", table["y"][1]),
            ],
            scratch=[pltpu.VMEM((BLOCKS, 8, 128), F32)],
        )
        held = exchange(spectrum)
        turned = atoms[:4].reshape(4, GROUPS, 32).transpose(0, 2, 1).reshape(128, GROUPS)
        near, halo = call(
            nonbonded_kernel,
            [shape(3, ATOMS), shape(8, 128)],
            [("s", place), ("v", atoms), ("v", turned), ("v", cluster_pairs), ("v", beyond)],
            scratch=[
                pltpu.VMEM((16, ATOMS), F32),
                pltpu.VMEM((128, ATOMS), F32),
                pltpu.VMEM((128, 128), F32),
            ],
            flops=8_000_000_000,
        )
        halo_back = permuted(halo, "dom", 1)
        filtered = call(
            filter_kernel,
            shape(DEVICES * MODES, 128),
            [
                ("s", place), ("s", table["y_square"]), ("s", table["y_factor"]), ("v", held),
                ("v", table["x"][0]), ("v", table["x"][1]),
                ("v", table["z"][0]), ("v", table["z"][1]),
                ("v", table["z_back"][0]), ("v", table["z_back"][1]),
                ("v", table["x_square"]), ("v", table["x_factor"]),
                ("v", table["z_square"]), ("v", table["z_factor"]),
            ],
            scratch=[pltpu.VMEM((MODES * NZ, N_DOM * XW), F32)],
        )
        returned = exchange(filtered)
        grid, rest = call(
            gather_rest_kernel,
            [shape(BLOCKS, 8, 128), shape(3, ATOMS)],
            [
                ("s", place), ("s", ya_behind), ("v", behind), ("v", returned),
                ("v", table["y_back"][0]), ("v", table["y_back"][1]),
            ],
        )
        rest_back = permuted(rest, "pme", -1)
        forces = call(
            gather_own_kernel,
            shape(3, ATOMS),
            [
                ("s", place), ("s", ya), ("v", atoms), ("v", grid), ("v", near),
                ("v", halo_back),
            ],
            flops=3_000_000_000,
        )
        return forces + rest_back

    return shards


def solution(mesh):
    in_specs = (
        P(("pme", "dom"), None),
        P(None, ("pme", "dom")),
        P(None, ("pme", "dom")),
        P(None, ("pme", "dom")),
        P(("pme", "dom")),
        P(None, ("pme", "dom")),
    )
    out_specs = P(None, ("pme", "dom"))
    return jax.shard_map(
        make_shards(tables()), mesh=mesh, in_specs=in_specs, out_specs=out_specs, check_vma=False
    )
```

```python
import math

import jax
import jax.numpy as jnp
import ml_dtypes
import numpy as np
from jax import lax
from jax.experimental import pallas as pl
from jax.experimental.pallas import tpu as pltpu
from jax.sharding import PartitionSpec as P

NX = 768
NY = 768
NZ = 32
N_DOM = 32
N_PME = 8
DEVICES = 256
XD = 24
YP = 24
ZP = 4
GROUPS = 64
ATOMS = 2048
PAIRS = 1024
CLUSTERS = 256
HALO_CLUSTERS = 8
HALO_ATOMS = 64
XW = 32
MODES = 3
BLOCKS = 98
BETA = 0.35
VMEM_LIMIT = 24 * 1024 * 1024

F32 = jnp.float32
BF16 = jnp.bfloat16

ERFC_Q = (
    0.2820947951,
    0.2820937768,
    0.2468838798,
    0.1753240754,
    0.0934147485,
    -0.05905091002,
    0.1318500403,
    -0.4545637183,
    0.493385742,
    -0.2346054907,
    0.04317306594,
)


def real_basis(length):
    point = np.arange(length)
    rows = np.zeros((length, length))
    waves = np.zeros(length, np.int64)
    rows[0] = 1.0 / math.sqrt(length)
    for k in range(1, length // 2):
        angle = 2.0 * math.pi * (k * point % length) / length
        rows[2 * k - 1] = math.sqrt(2.0 / length) * np.cos(angle)
        rows[2 * k] = math.sqrt(2.0 / length) * np.sin(angle)
        waves[2 * k - 1] = k
        waves[2 * k] = k
    rows[length - 1] = (1.0 - 2.0 * (point % 2)) / math.sqrt(length)
    waves[length - 1] = length // 2
    order = np.argsort(waves % 2, kind="stable")
    return rows[order], waves[order]


def wave_factors(waves, length):
    freq = waves / length
    modulus = 1.0 / (2.0 / 3.0 + np.cos(2.0 * math.pi * waves / length) / 3.0) ** 2
    return freq * freq, np.exp(-((math.pi / BETA) ** 2) * freq * freq) * modulus


def halves(table):
    table = table.astype(np.float32)
    high = table.astype(ml_dtypes.bfloat16)
    low = (table - high.astype(np.float32)).astype(ml_dtypes.bfloat16)
    return high, low


def split(value):
    high = value.astype(BF16)
    low = (value - high.astype(F32)).astype(BF16)
    return high, low


def dot(a, b):
    return jnp.dot(a, b, preferred_element_type=F32)


def dot_nt(a, b):
    return lax.dot_general(a, b, (((1,), (1,)), ((), ())), preferred_element_type=F32)


def dot_tn(a, b):
    return lax.dot_general(a, b, (((0,), (0,)), ((), ())), preferred_element_type=F32)


def times_table(table_high, table_low, value):
    high, low = split(value)
    both = dot(table_high, jnp.concatenate([high, low], axis=1))
    return both[:, :128] + (both[:, 128:] + dot(table_low, high))


def iota(shape, dim):
    return lax.broadcasted_iota(jnp.int32, shape, dim)


def spline(u):
    d = jnp.abs(u)
    a = jnp.maximum(2.0 - d, 0.0)
    b = jnp.maximum(1.0 - d, 0.0)
    return (a * a * a - 4.0 * (b * b * b)) * (1.0 / 6.0)


def spline_slope(u):
    d = jnp.abs(u)
    a = jnp.maximum(2.0 - d, 0.0)
    b = jnp.maximum(1.0 - d, 0.0)
    slope = 0.5 * (a * a) - 2.0 * (b * b)
    return slope, (a * a * a - 4.0 * (b * b * b)) * (1.0 / 6.0)


def weights_of(u):
    slope, value = spline_slope(u)
    return value, jnp.where(u < 0.0, -slope, slope)


def prepare_kernel(
    col_in, corner_in, cell_in, fraction_in, charge_in, atoms, edge,
    col, corner, cell, fraction, charge, arrived,
):
    copies = [
        pltpu.make_async_copy(source, target, arrived.at[i])
        for i, (source, target) in enumerate(
            (
                (col_in, col), (corner_in, corner), (cell_in, cell),
                (fraction_in, fraction), (charge_in, charge),
            )
        )
    ]
    for copy in copies:
        copy.start()
    for copy in copies:
        copy.wait()
    group = iota((GROUPS, ATOMS), 0)
    hot = jnp.where((iota((GROUPS, ATOMS), 1) >> 5) == group, 1.0, 0.0).astype(BF16)
    rep_corner = dot(corner[...].astype(F32).astype(BF16), hot)
    rep_col = dot(
        jnp.broadcast_to(col[...].astype(F32), (8, GROUPS)).astype(BF16), hot
    )[0:1]
    base = rep_corner + cell[...].astype(F32)
    first = (lax.axis_index("dom") * XD).astype(F32)
    third = (lax.axis_index("pme") * ZP).astype(F32)
    along_x = (base[0:1] + first) + fraction[0:1, :]
    along_y = (base[1:2] + rep_col * float(YP)) + fraction[1:2, :]
    along_z = (base[2:3] + third) + fraction[2:3, :]
    atoms[...] = jnp.zeros((8, ATOMS), F32)
    atoms[0:1, :] = along_x
    atoms[1:2, :] = along_y
    atoms[2:3, :] = along_z
    atoms[3:4, :] = charge[...]
    lowest = (col[...] * YP + corner[1:2, :]).astype(F32)
    atoms[4:5, 0:GROUPS] = lowest
    edge[...] = atoms[:, 0:128]


def y_blocks(ya, batch, lane):
    starts = [ya[4 * batch + j] for j in range(4)]
    row = jnp.where(
        lane < 64,
        jnp.where(lane < 32, starts[0], starts[1]),
        jnp.where(lane < 96, starts[2], starts[3]),
    )
    return starts, (row * 8).astype(F32)


def masked_blocks(weights, lane):
    return jnp.concatenate(
        [jnp.where((lane >> 5) == j, weights, 0.0) for j in range(4)], axis=0
    )


def spread_batches(origin_x, origin_z, ya, atoms, grid):
    lane = iota((1, 128), 1)
    step_x = iota((XW, 128), 0).astype(F32)
    step_y = iota((24, 128), 0).astype(F32)
    step_z = iota((8, 128), 0).astype(F32)
    for batch in range(ATOMS // 128):
        own = slice(128 * batch, 128 * batch + 128)
        starts, base_y = y_blocks(ya, batch, lane)
        xs = (atoms[0:1, own] - origin_x) + 1.0
        ys = (atoms[1:2, own] - base_y) + 1.0
        zs = (atoms[2:3, own] - origin_z) + 1.0
        wx = spline(step_x - xs)
        wz = spline(step_z - zs) * atoms[3:4, own]
        wy = masked_blocks(spline(step_y - ys), lane)
        charged = jnp.concatenate([wx * wz[z : z + 1] for z in range(ZP)], axis=0)
        c_high, c_low = split(charged)
        y_high, y_low = split(wy)
        added = dot_nt(
            jnp.concatenate([y_high, y_low], axis=1), jnp.concatenate([c_high, c_high], axis=1)
        ) + dot_nt(y_high, c_low)
        for j in range(4):
            part = added[24 * j : 24 * j + 24].reshape(3, 8, 128)
            grid[pl.ds(starts[j], 3)] = grid[pl.ds(starts[j], 3)] + part


def spread_own_kernel(ya, atoms, grid):
    grid[...] = jnp.zeros((BLOCKS, 8, 128), F32)
    origin_x = (lax.axis_index("dom") * XD).astype(F32)
    origin_z = (lax.axis_index("pme") * ZP).astype(F32)
    spread_batches(origin_x, origin_z, ya, atoms, grid)


def neighbour_origin():
    behind = (lax.axis_index("pme") + (N_PME - 1)) & (N_PME - 1)
    return (lax.axis_index("dom") * XD).astype(F32), (behind * ZP + ZP).astype(F32)


def spread_rest_kernel(ya, atoms, own, even_high, even_low, odd_high, odd_low, out, grid):
    grid[...] = own[...]
    origin_x, origin_z = neighbour_origin()
    spread_batches(origin_x, origin_z, ya, atoms, grid)
    grid[0:2] = grid[0:2] + grid[96:98]
    lower = grid[0:48].reshape(NY // 2, 128)
    upper = grid[48:96].reshape(NY // 2, 128)
    out[0 : NY // 2, :] = times_table(even_high[...], even_low[...], lower + upper)
    out[NY // 2 :, :] = times_table(odd_high[...], odd_low[...], lower - upper)


def filter_kernel(
    y_info, held, even_high, even_low, odd_high, odd_low, kz_high, kz_low, tz_high, tz_low,
    x_square, x_factor, z_square, z_factor, out, work,
):
    lane = iota((8, 128), 1) >> 5
    for m in range(MODES):
        for a in range(8):
            blocks = [held[pl.ds((4 * a + b) * 24 + m, 8, stride=3), :] for b in range(4)]
            for z in range(ZP):
                tile = None
                for b in range(4):
                    shift = (32 * (b - z)) % 128
                    moved = blocks[b] if shift == 0 else pltpu.roll(blocks[b], shift, 1)
                    tile = moved if tile is None else jnp.where(lane == b, moved, tile)
                row = m * NZ + z * 8
                work[row : row + 8, 128 * a : 128 * a + 128] = tile
    rows = MODES * NZ
    half = N_DOM // 2 * XW
    lower, upper = work[:, :half], work[:, half:]
    waves = []
    for value, high, low in ((lower + upper, even_high, even_low), (lower - upper, odd_high, odd_low)):
        v_high, v_low = split(value)
        both = dot(jnp.concatenate([v_high, v_low], axis=0), high[...])
        waves.append(both[:rows] + (both[rows:] + dot(v_high, low[...])))
    w_high, w_low = split(jnp.concatenate(waves, axis=1))
    full = dot(kz_high[...], w_high) + (dot(kz_high[...], w_low) + dot(kz_low[...], w_high))
    device = lax.axis_index("dom") * N_PME + lax.axis_index("pme")
    info = y_info[pl.ds(device, 1), :]
    scaled = []
    for m in range(MODES):
        square = (x_square[...] + z_square[:, 0:1]) + info[:, m : m + 1]
        factor = (x_factor[...] * z_factor[:, 0:1]) * info[:, MODES + m : MODES + m + 1]
        nonzero = jnp.where(square > 0.0, square, 1.0)
        influence = jnp.where(square > 0.0, factor / nonzero, 0.0)
        scaled.append(full[m * NZ : m * NZ + NZ] * influence)
    s_high, s_low = split(jnp.concatenate(scaled, axis=0))
    back = dot(tz_high[...], s_high) + (dot(tz_high[...], s_low) + dot(tz_low[...], s_high))
    parts = []
    for value, high, low in (
        (back[:, : NX // 2], even_high, even_low), (back[:, NX // 2 :], odd_high, odd_low),
    ):
        v_high, v_low = split(value)
        both = dot_nt(jnp.concatenate([v_high, v_low], axis=0), high[...])
        parts.append(both[:rows] + (both[rows:] + dot_nt(v_high, low[...])))
    work[:, :half] = parts[0] + parts[1]
    work[:, half:] = parts[0] - parts[1]
    for m in range(MODES):
        for a in range(8):
            tiles = [
                work[m * NZ + z * 8 : m * NZ + z * 8 + 8, 128 * a : 128 * a + 128]
                for z in range(ZP)
            ]
            for b in range(4):
                block = None
                for z in range(ZP):
                    shift = (32 * (z - b)) % 128
                    moved = tiles[z] if shift == 0 else pltpu.roll(tiles[z], shift, 1)
                    block = moved if block is None else jnp.where(lane == z, moved, block)
                out[pl.ds((4 * a + b) * 24 + m, 8, stride=3), :] = block


def gather_batches(origin_x, origin_z, ya, atoms, grid, store):
    lane = iota((1, 128), 1)
    step_x = iota((XW, 128), 0).astype(F32)
    step_y = iota((24, 128), 0).astype(F32)
    step_z = iota((8, 128), 0).astype(F32)
    for batch in range(ATOMS // 128):
        own = slice(128 * batch, 128 * batch + 128)
        starts, base_y = y_blocks(ya, batch, lane)
        xs = (atoms[0:1, own] - origin_x) + 1.0
        ys = (atoms[1:2, own] - base_y) + 1.0
        zs = (atoms[2:3, own] - origin_z) + 1.0
        wx, sx = weights_of(step_x - xs)
        wy, sy = weights_of(step_y - ys)
        wz, sz = weights_of(step_z - zs)
        block = jnp.concatenate(
            [grid[pl.ds(starts[j], 3)].reshape(24, 128) for j in range(4)], axis=0
        )
        b_high, b_low = split(block)
        y_both = jnp.concatenate([masked_blocks(wy, lane), masked_blocks(sy, lane)], axis=1)
        y_high, y_low = split(y_both)
        sampled = dot_tn(
            jnp.concatenate([b_high, b_low], axis=0), jnp.concatenate([y_high, y_high], axis=0)
        ) + dot_tn(b_high, y_low)
        along_x = along_y = along_z = jnp.zeros((XW, 128), F32)
        for z in range(ZP):
            value = sampled[XW * z : XW * z + XW, :128]
            slope = sampled[XW * z : XW * z + XW, 128:]
            along_x = along_x + value * wz[z : z + 1]
            along_y = along_y + slope * wz[z : z + 1]
            along_z = along_z + value * sz[z : z + 1]
        minus = -atoms[3:4, own]
        store(
            own,
            minus * jnp.sum(along_x * sx, axis=0, keepdims=True),
            minus * jnp.sum(along_y * wx, axis=0, keepdims=True),
            minus * jnp.sum(along_z * wx, axis=0, keepdims=True),
        )


def gather_rest_kernel(ya, atoms, held, even_high, even_low, odd_high, odd_low, grid, out):
    even = times_table(even_high[...], even_low[...], held[0 : NY // 2, :])
    odd = times_table(odd_high[...], odd_low[...], held[NY // 2 :, :])
    grid[0:48] = (even + odd).reshape(48, 8, 128)
    grid[48:96] = (even - odd).reshape(48, 8, 128)
    grid[96:98] = grid[0:2]
    origin_x, origin_z = neighbour_origin()

    def store(own, fx, fy, fz):
        out[0:1, own] = fx
        out[1:2, own] = fy
        out[2:3, own] = fz

    gather_batches(origin_x, origin_z, ya, atoms, grid, store)


def gather_own_kernel(ya, atoms, grid, near, halo, out):
    origin_x = (lax.axis_index("dom") * XD).astype(F32)
    origin_z = (lax.axis_index("pme") * ZP).astype(F32)

    def store(own, fx, fy, fz):
        forces = [fx, fy, fz]
        for f in range(3):
            total = forces[f] + near[f : f + 1, own]
            if own.start == 0:
                total = total + halo[f : f + 1, :]
            out[f : f + 1, own] = total

    gather_batches(origin_x, origin_z, ya, atoms, grid, store)


def pair_strength(dist_sq):
    inverse = lax.rsqrt(dist_sq)
    inverse = inverse * (1.5 - 0.5 * dist_sq * inverse * inverse)
    scaled = BETA * (dist_sq * inverse)
    t = 1.0 / (1.0 + 0.5 * scaled)
    poly = jnp.full_like(t, ERFC_Q[-1])
    for coefficient in ERFC_Q[-2::-1]:
        poly = poly * t + coefficient
    fall = jnp.exp(-(BETA * BETA) * dist_sq)
    bracket = t * poly * inverse + 2.0 * BETA / math.sqrt(math.pi)
    return fall * bracket * (inverse * inverse)


def nonbonded_kernel(atoms, turned, pairs, beyond, near, halo, weight, repeated, columns):
    left = pairs[0:1, :]
    right = pairs[1:2, :]
    inside = right < CLUSTERS
    cluster = iota((CLUSTERS, PAIRS), 0)
    hot_left = jnp.where(cluster == left, 1.0, 0.0).astype(BF16)
    hot_right = jnp.where(cluster == right, 1.0, 0.0).astype(BF16)
    code = iota((16, PAIRS), 0)
    code_left = jnp.where(
        code == jnp.where(inside, right & 3, right - (CLUSTERS - 4)), 1.0, 0.0
    ).astype(BF16)
    code_right = jnp.where(
        code == jnp.where(inside, left & 3, -1), 1.0, 0.0
    ).astype(BF16)
    count = dot_nt(code_left, hot_left) + dot_nt(code_right, hot_right)
    n_high, n_low = split(count)
    expand = jnp.where(
        (iota((CLUSTERS, ATOMS), 1) >> 3) == iota((CLUSTERS, ATOMS), 0), 1.0, 0.0
    ).astype(BF16)
    weight[...] = dot(n_high, expand) + dot(n_low, expand)
    turn_1 = turned[...].astype(BF16)
    rest = turned[...] - turn_1.astype(F32)
    turn_2 = rest.astype(BF16)
    turn_3 = (rest - turn_2.astype(F32)).astype(BF16)
    spreading = jnp.where(
        (iota((GROUPS, ATOMS), 1) >> 5) == iota((GROUPS, ATOMS), 0), 1.0, 0.0
    ).astype(BF16)
    repeated[...] = (dot(turn_1, spreading) + dot(turn_2, spreading)) + dot(turn_3, spreading)
    row = iota((8, 128), 0)
    lane = iota((8, 128), 1)
    for tile in range(ATOMS // 128):
        own = slice(128 * tile, 128 * tile + 128)
        px, py, pz = atoms[0:1, own], atoms[1:2, own], atoms[2:3, own]
        sum_x = sum_y = sum_z = jnp.zeros((8, 128), F32)
        for i in range(4):
            dx = px - repeated[8 * i : 8 * i + 8, own]
            dy = py - repeated[32 + 8 * i : 40 + 8 * i, own]
            dz = pz - repeated[64 + 8 * i : 72 + 8 * i, own]
            other = repeated[96 + 8 * i : 104 + 8 * i, own]
            dist_sq = (dx * dx + dy * dy) + dz * dz
            itself = (lane & 31) == (row + 8 * i)
            dist_sq = jnp.where(itself, 1.0, dist_sq)
            strength = pair_strength(dist_sq) * (other * weight[i : i + 1, own])
            sum_x = sum_x + strength * dx
            sum_y = sum_y + strength * dy
            sum_z = sum_z + strength * dz
        near[0:1, own] = jnp.sum(sum_x, axis=0, keepdims=True)
        near[1:2, own] = jnp.sum(sum_y, axis=0, keepdims=True)
        near[2:3, own] = jnp.sum(sum_z, axis=0, keepdims=True)
    lift = jnp.where(lax.axis_index("dom") == N_DOM - 1, float(NX), 0.0)
    upright = jnp.transpose(jnp.concatenate([beyond[...]] * 16, axis=0))
    columns[...] = jnp.zeros((128, 128), F32)
    for c in range(HALO_CLUSTERS):
        part = upright[8 * c : 8 * c + 8]
        hx = part[:, 0:1] + lift
        hy = part[:, 1:2]
        hz = part[:, 2:3]
        hq = part[:, 3:4]
        sum_x = sum_y = sum_z = jnp.zeros((8, 128), F32)
        for tile in range(ATOMS // 128):
            own = slice(128 * tile, 128 * tile + 128)
            dx = atoms[0:1, own] - hx
            dy = atoms[1:2, own] - hy
            dz = atoms[2:3, own] - hz
            dist_sq = (dx * dx + dy * dy) + dz * dz
            both = weight[4 + c : 5 + c, own]
            strength = pair_strength(dist_sq) * both
            on_own = strength * hq
            near[0:1, own] = near[0:1, own] + jnp.sum(on_own * dx, axis=0, keepdims=True)
            near[1:2, own] = near[1:2, own] + jnp.sum(on_own * dy, axis=0, keepdims=True)
            near[2:3, own] = near[2:3, own] + jnp.sum(on_own * dz, axis=0, keepdims=True)
            on_halo = strength * atoms[3:4, own]
            sum_x = sum_x - on_halo * dx
            sum_y = sum_y - on_halo * dy
            sum_z = sum_z - on_halo * dz
        force_x = jnp.sum(sum_x, axis=1, keepdims=True) * hq
        force_y = jnp.sum(sum_y, axis=1, keepdims=True) * hq
        force_z = jnp.sum(sum_z, axis=1, keepdims=True) * hq
        columns[8 * c : 8 * c + 8, :] = jnp.where(
            lane == 0, force_x, jnp.where(lane == 1, force_y, jnp.where(lane == 2, force_z, 0.0))
        )
    halo[...] = jnp.transpose(columns[...])[0:8]
    for f in range(3):
        near[f : f + 1, :] = near[f : f + 1, :] * atoms[3:4, :]


def call(kernel, outs, ins, scratch=(), flops=1_000_000):
    vmem = pl.BlockSpec(memory_space=pltpu.VMEM)
    smem = pl.BlockSpec(memory_space=pltpu.SMEM)
    spaces = {"s": smem, "v": vmem, "h": pl.BlockSpec(memory_space=pltpu.HBM)}
    in_specs = [spaces[kind] for kind, _ in ins]
    many = isinstance(outs, list)
    return pl.pallas_call(
        kernel,
        out_shape=outs,
        in_specs=in_specs,
        out_specs=[vmem] * len(outs) if many else vmem,
        scratch_shapes=list(scratch),
        compiler_params=pltpu.CompilerParams(vmem_limit_bytes=VMEM_LIMIT),
        cost_estimate=pl.CostEstimate(flops=flops, bytes_accessed=1_000_000, transcendentals=0),
    )(*[x for _, x in ins])


def shape(*dims):
    return jax.ShapeDtypeStruct(dims, F32)


def permuted(x, axis, by):
    length = lax.axis_size(axis)
    return lax.ppermute(x, axis, [(i, (i + by) % length) for i in range(length)])


def exchange(x):
    sent = x.reshape(DEVICES, 1, MODES * 128)
    return lax.all_to_all(sent, ("dom", "pme"), 0, 0).reshape(DEVICES * MODES, 128)


def tables():
    along_y, y_waves = real_basis(NY)
    along_x, x_waves = real_basis(NX)
    along_z, z_waves = real_basis(NZ)
    folded = np.zeros((N_DOM * XW, NX))
    for q in range(N_DOM):
        for x in range(XD + 3):
            folded[q * XW + x] = along_x[:, (q * XD + x) % NX]
    order = np.array([4 * p + z for z in range(ZP) for p in range(N_PME)])
    z_rows = np.kron(np.eye(MODES), along_z[:, order])
    y_square, y_factor = wave_factors(y_waves, NY)
    y_info = np.zeros((DEVICES, 128))
    y_info[:, 0:MODES] = y_square.reshape(DEVICES, MODES)
    y_info[:, MODES : 2 * MODES] = y_factor.reshape(DEVICES, MODES)
    x_square, x_factor = wave_factors(x_waves, NX)
    z_square, z_factor = wave_factors(z_waves, NZ)
    f32 = np.float32
    return {
        "y_even": halves(along_y[: NY // 2, : NY // 2]),
        "y_odd": halves(along_y[NY // 2 :, : NY // 2]),
        "y_even_back": halves(along_y[: NY // 2, : NY // 2].T),
        "y_odd_back": halves(along_y[NY // 2 :, : NY // 2].T),
        "x_even": halves(folded[: N_DOM // 2 * XW, : NX // 2]),
        "x_odd": halves(folded[: N_DOM // 2 * XW, NX // 2 :]),
        "z": halves(z_rows),
        "z_back": halves(z_rows.T),
        "y_info": y_info.astype(f32),
        "x_square": x_square.astype(f32)[None, :],
        "x_factor": (x_factor / math.pi).astype(f32)[None, :],
        "z_square": np.repeat(z_square.astype(f32)[:, None], 128, axis=1),
        "z_factor": np.repeat(z_factor.astype(f32)[:, None], 128, axis=1),
    }


def make_shards(table):
    def shards(group_column, group_corner, atom_cell, fraction, charge, cluster_pairs):
        column = group_column.reshape(1, GROUPS)
        atoms, edge = call(
            prepare_kernel,
            [shape(8, ATOMS), shape(8, 128)],
            [
                ("h", pltpu.with_memory_space_constraint(column, pltpu.HBM)),
                ("h", pltpu.with_memory_space_constraint(group_corner, pltpu.HBM)),
                ("h", pltpu.with_memory_space_constraint(atom_cell, pltpu.HBM)),
                ("h", pltpu.with_memory_space_constraint(fraction, pltpu.HBM)),
                ("h", pltpu.with_memory_space_constraint(charge.reshape(1, ATOMS), pltpu.HBM)),
            ],
            scratch=[
                pltpu.VMEM((1, GROUPS), jnp.int32),
                pltpu.VMEM((3, GROUPS), jnp.int32),
                pltpu.VMEM((3, ATOMS), jnp.int32),
                pltpu.VMEM((3, ATOMS), F32),
                pltpu.VMEM((1, ATOMS), F32),
                pltpu.SemaphoreType.DMA((5,)),
            ],
        )
        behind = permuted(atoms, "pme", 1)
        beyond = permuted(edge, "dom", -1)
        ya = (column[0] * YP + group_corner[1]) >> 3
        own_grid = call(
            spread_own_kernel,
            shape(BLOCKS, 8, 128),
            [("s", ya), ("v", atoms)],
            flops=3_000_000_000,
        )
        ya_behind = behind[4, :GROUPS].astype(jnp.int32) >> 3
        spectrum = call(
            spread_rest_kernel,
            shape(NY, 128),
            [
                ("s", ya_behind), ("v", behind), ("v", own_grid),
                *[("v", x) for x in table["y_even"] + table["y_odd"]],
            ],
            scratch=[pltpu.VMEM((BLOCKS, 8, 128), F32)],
        )
        held = exchange(spectrum)
        turned = atoms[:4].reshape(4, GROUPS, 32).transpose(0, 2, 1).reshape(128, GROUPS)
        near, halo = call(
            nonbonded_kernel,
            [shape(3, ATOMS), shape(8, 128)],
            [("v", atoms), ("v", turned), ("v", cluster_pairs), ("v", beyond)],
            scratch=[
                pltpu.VMEM((16, ATOMS), F32),
                pltpu.VMEM((128, ATOMS), F32),
                pltpu.VMEM((128, 128), F32),
            ],
            flops=8_000_000_000,
        )
        halo_back = permuted(halo, "dom", 1)
        filtered = call(
            filter_kernel,
            shape(DEVICES * MODES, 128),
            [
                ("v", table["y_info"]), ("v", held),
                *[("v", x) for x in table["x_even"] + table["x_odd"]],
                ("v", table["z"][0]), ("v", table["z"][1]),
                ("v", table["z_back"][0]), ("v", table["z_back"][1]),
                ("v", table["x_square"]), ("v", table["x_factor"]),
                ("v", table["z_square"]), ("v", table["z_factor"]),
            ],
            scratch=[pltpu.VMEM((MODES * NZ, N_DOM * XW), F32)],
        )
        returned = exchange(filtered)
        grid, rest = call(
            gather_rest_kernel,
            [shape(BLOCKS, 8, 128), shape(3, ATOMS)],
            [
                ("s", ya_behind), ("v", behind), ("v", returned),
                *[("v", x) for x in table["y_even_back"] + table["y_odd_back"]],
            ],
        )
        rest_back = permuted(rest, "pme", -1)
        forces = call(
            gather_own_kernel,
            shape(3, ATOMS),
            [
                ("s", ya), ("v", atoms), ("v", grid), ("v", near),
                ("v", halo_back),
            ],
            flops=3_000_000_000,
        )
        return forces + rest_back

    return shards


def solution(mesh):
    in_specs = (
        P(("pme", "dom"), None),
        P(None, ("pme", "dom")),
        P(None, ("pme", "dom")),
        P(None, ("pme", "dom")),
        P(("pme", "dom")),
        P(None, ("pme", "dom")),
    )
    out_specs = P(None, ("pme", "dom"))
    return jax.shard_map(
        make_shards(tables()), mesh=mesh, in_specs=in_specs, out_specs=out_specs, check_vma=False
    )
```

```python
import math

import jax
import jax.numpy as jnp
import ml_dtypes
import numpy as np
from jax import lax
from jax.experimental import pallas as pl
from jax.experimental.pallas import tpu as pltpu
from jax.sharding import PartitionSpec as P

NX = 768
NY = 768
NZ = 32
N_DOM = 32
N_PME = 8
DEVICES = 256
XD = 24
YP = 24
ZP = 4
GROUPS = 64
ATOMS = 2048
CARRIED = ATOMS + 128
PAIRS = 1024
CLUSTERS = 256
HALO_CLUSTERS = 8
HALO_ATOMS = 64
XW = 32
MODES = 3
LOW_Y = 64
LOW_X = 128
BLOCKS = 98
BETA = 0.35
VMEM_LIMIT = 24 * 1024 * 1024

F32 = jnp.float32
BF16 = jnp.bfloat16

ERFC_Q = (
    0.2820947951,
    0.2820937768,
    0.2468838798,
    0.1753240754,
    0.0934147485,
    -0.05905091002,
    0.1318500403,
    -0.4545637183,
    0.493385742,
    -0.2346054907,
    0.04317306594,
)


def real_basis(length):
    point = np.arange(length)
    rows = np.zeros((length, length))
    waves = np.zeros(length, np.int64)
    rows[0] = 1.0 / math.sqrt(length)
    for k in range(1, length // 2):
        angle = 2.0 * math.pi * (k * point % length) / length
        rows[2 * k - 1] = math.sqrt(2.0 / length) * np.cos(angle)
        rows[2 * k] = math.sqrt(2.0 / length) * np.sin(angle)
        waves[2 * k - 1] = k
        waves[2 * k] = k
    rows[length - 1] = (1.0 - 2.0 * (point % 2)) / math.sqrt(length)
    waves[length - 1] = length // 2
    order = np.argsort(waves % 2, kind="stable")
    return rows[order], waves[order]


def wave_factors(waves, length):
    freq = waves / length
    modulus = 1.0 / (2.0 / 3.0 + np.cos(2.0 * math.pi * waves / length) / 3.0) ** 2
    return freq * freq, np.exp(-((math.pi / BETA) ** 2) * freq * freq) * modulus


def halves(table):
    table = table.astype(np.float32)
    high = table.astype(ml_dtypes.bfloat16)
    low = (table - high.astype(np.float32)).astype(ml_dtypes.bfloat16)
    return high, low


def thirds(table, axis):
    table = table.astype(np.float32)
    high, middle = halves(table)
    low = (table - high.astype(np.float32)) - middle.astype(np.float32)
    return np.concatenate([low.astype(ml_dtypes.bfloat16), high, middle], axis=axis)


def finest(value, axis):
    high = value.astype(BF16)
    rest = value - high.astype(F32)
    middle = rest.astype(BF16)
    low = (rest - middle.astype(F32)).astype(BF16)
    return jnp.concatenate([high, low, middle], axis=axis)


def split(value):
    high = value.astype(BF16)
    low = (value - high.astype(F32)).astype(BF16)
    return high, low


def dot(a, b):
    return jnp.dot(a, b, preferred_element_type=F32)


def dot_nt(a, b):
    return lax.dot_general(a, b, (((1,), (1,)), ((), ())), preferred_element_type=F32)


def dot_tn(a, b):
    return lax.dot_general(a, b, (((0,), (0,)), ((), ())), preferred_element_type=F32)


def times_table(table_high, table_low, value):
    high, low = split(value)
    both = dot(table_high, jnp.concatenate([high, low], axis=1))
    return both[:, :128] + (both[:, 128:] + dot(table_low, high))


def iota(shape, dim):
    return lax.broadcasted_iota(jnp.int32, shape, dim)


def spline(u):
    d = jnp.abs(u)
    a = jnp.maximum(2.0 - d, 0.0)
    b = jnp.maximum(1.0 - d, 0.0)
    return (a * a * a - 4.0 * (b * b * b)) * (1.0 / 6.0)


def spline_slope(u):
    d = jnp.abs(u)
    a = jnp.maximum(2.0 - d, 0.0)
    b = jnp.maximum(1.0 - d, 0.0)
    slope = 0.5 * (a * a) - 2.0 * (b * b)
    return slope, (a * a * a - 4.0 * (b * b * b)) * (1.0 / 6.0)


def weights_of(u):
    slope, value = spline_slope(u)
    return value, jnp.where(u < 0.0, -slope, slope)


def prepare_kernel(
    col_in, corner_in, cell_in, fraction_in, charge_in, atoms, edge,
    col, corner, cell, fraction, charge, arrived,
):
    copies = [
        pltpu.make_async_copy(source, target, arrived.at[i])
        for i, (source, target) in enumerate(
            (
                (col_in, col), (corner_in, corner), (cell_in, cell),
                (fraction_in, fraction), (charge_in, charge),
            )
        )
    ]
    for copy in copies:
        copy.start()
    for copy in copies:
        copy.wait()
    group = iota((GROUPS, ATOMS), 0)
    hot = jnp.where((iota((GROUPS, ATOMS), 1) >> 5) == group, 1.0, 0.0).astype(BF16)
    rep_corner = dot(corner[...].astype(F32).astype(BF16), hot)
    rep_col = dot(
        jnp.broadcast_to(col[...].astype(F32), (8, GROUPS)).astype(BF16), hot
    )[0:1]
    base = rep_corner + cell[...].astype(F32)
    first = (lax.axis_index("dom") * XD).astype(F32)
    third = (lax.axis_index("pme") * ZP).astype(F32)
    along_x = (base[0:1] + first) + fraction[0:1, :]
    along_y = (base[1:2] + rep_col * float(YP)) + fraction[1:2, :]
    along_z = (base[2:3] + third) + fraction[2:3, :]
    atoms[0:1, 0:ATOMS] = along_x
    atoms[1:2, 0:ATOMS] = along_y
    atoms[2:3, 0:ATOMS] = along_z
    atoms[3:4, 0:ATOMS] = charge[...]
    atoms[:, ATOMS:] = jnp.zeros((4, 128), F32)
    lowest = (col[...] * YP + corner[1:2, :]).astype(F32)
    atoms[0:1, ATOMS : ATOMS + GROUPS] = lowest
    edge[...] = atoms[:, 0:128]


def y_blocks(ya, batch, lane):
    starts = [ya[4 * batch + j] for j in range(4)]
    row = jnp.where(
        lane < 64,
        jnp.where(lane < 32, starts[0], starts[1]),
        jnp.where(lane < 96, starts[2], starts[3]),
    )
    return starts, (row * 8).astype(F32)


def masked_blocks(weights, lane):
    return jnp.concatenate(
        [jnp.where((lane >> 5) == j, weights, 0.0) for j in range(4)], axis=0
    )


def spread_batches(origin_x, origin_z, planes, ya, atoms, grid):
    lane = iota((1, 128), 1)
    step_x = iota((XW, 128), 0).astype(F32)
    step_y = iota((24, 128), 0).astype(F32)
    step_z = iota((8, 128), 0).astype(F32)
    for batch in range(ATOMS // 128):
        own = slice(128 * batch, 128 * batch + 128)
        starts, base_y = y_blocks(ya, batch, lane)
        xs = (atoms[0:1, own] - origin_x) + 1.0
        ys = (atoms[1:2, own] - base_y) + 1.0
        zs = (atoms[2:3, own] - origin_z) + 1.0
        wx = spline(step_x - xs)
        wz = spline(step_z - zs) * atoms[3:4, own]
        wy = masked_blocks(spline(step_y - ys), lane)
        charged = jnp.concatenate([wx * wz[z : z + 1] for z in range(planes)], axis=0)
        c_high, c_low = split(charged)
        y_high, y_low = split(wy)
        added = dot_nt(
            jnp.concatenate([y_high, y_low], axis=1), jnp.concatenate([c_high, c_high], axis=1)
        ) + dot_nt(y_high, c_low)
        for j in range(4):
            part = added[24 * j : 24 * j + 24].reshape(3, 8, XW * planes)
            where = (pl.ds(starts[j], 3), slice(None), slice(0, XW * planes))
            grid[where] = grid[where] + part


def spread_own_kernel(ya, atoms, grid):
    grid[...] = jnp.zeros((BLOCKS, 8, 128), F32)
    origin_x = (lax.axis_index("dom") * XD).astype(F32)
    origin_z = (lax.axis_index("pme") * ZP).astype(F32)
    spread_batches(origin_x, origin_z, ZP, ya, atoms, grid)


def neighbour_origin():
    behind = (lax.axis_index("pme") + (N_PME - 1)) & (N_PME - 1)
    return (lax.axis_index("dom") * XD).astype(F32), (behind * ZP + ZP).astype(F32)


def spread_rest_kernel(ya, atoms, own, even_high, even_low, odd_high, odd_low, out, grid):
    grid[...] = own[...]
    origin_x, origin_z = neighbour_origin()
    spread_batches(origin_x, origin_z, ZP - 1, ya, atoms, grid)
    grid[0:2] = grid[0:2] + grid[96:98]
    lower = grid[0:48].reshape(NY // 2, 128)
    upper = grid[48:96].reshape(NY // 2, 128)
    out[0 : NY // 2, :] = times_table(even_high[...], even_low[...], lower + upper)
    out[NY // 2 :, :] = times_table(odd_high[...], odd_low[...], lower - upper)


def filter_kernel(
    y_info, held, even_high, even_low, odd_high, odd_low, even_fine, odd_fine, kz_high, kz_low, tz_high, tz_low, tz_fine,
    x_square, x_factor, z_square, z_factor, out, work,
):
    lane = iota((8, 128), 1) >> 5
    for m in range(MODES):
        for a in range(8):
            blocks = [held[pl.ds((4 * a + b) * 24 + m, 8, stride=3), :] for b in range(4)]
            for z in range(ZP):
                tile = None
                for b in range(4):
                    shift = (32 * (b - z)) % 128
                    moved = blocks[b] if shift == 0 else pltpu.roll(blocks[b], shift, 1)
                    tile = moved if tile is None else jnp.where(lane == b, moved, tile)
                row = m * NZ + z * 8
                work[row : row + 8, 128 * a : 128 * a + 128] = tile
    rows = MODES * NZ
    half = N_DOM // 2 * XW
    lower, upper = work[:, :half], work[:, half:]
    waves = []
    for value, high, low in ((lower + upper, even_high, even_low), (lower - upper, odd_high, odd_low)):
        v_high, v_low = split(value)
        both = dot(jnp.concatenate([v_high, v_low], axis=0), high[...])
        waves.append(both[:rows] + (both[rows:] + dot(v_high, low[...])))
    w_high, w_low = split(jnp.concatenate(waves, axis=1))
    full = dot(kz_high[...], w_high) + (dot(kz_high[...], w_low) + dot(kz_low[...], w_high))
    device = lax.axis_index("dom") * N_PME + lax.axis_index("pme")
    info = y_info[pl.ds(device, 1), :]
    scaled = []
    for m in range(MODES):
        square = (x_square[...] + z_square[:, 0:1]) + info[:, m : m + 1]
        factor = (x_factor[...] * z_factor[:, 0:1]) * info[:, MODES + m : MODES + m + 1]
        nonzero = jnp.where(square > 0.0, square, 1.0)
        influence = jnp.where(square > 0.0, factor / nonzero, 0.0)
        scaled.append(full[m * NZ : m * NZ + NZ] * influence)
    scaled = jnp.concatenate(scaled, axis=0)
    s_high, s_low = split(scaled)
    back = dot(tz_high[...], s_high) + (
        dot(tz_high[...], s_low)
        + (dot(tz_low[...], s_high) + dot(tz_fine[...], finest(scaled, 0)))
    )
    parts = []
    for value, high, low, fine in (
        (back[:, : NX // 2], even_high, even_low, even_fine),
        (back[:, NX // 2 :], odd_high, odd_low, odd_fine),
    ):
        v_high, v_low = split(value)
        both = dot_nt(jnp.concatenate([v_high, v_low], axis=0), high[...])
        small = dot_nt(v_high, low[...]) + dot_nt(finest(value[:, :LOW_X], 1), fine[...])
        parts.append(both[:rows] + (both[rows:] + small))
    work[:, :half] = parts[0] + parts[1]
    work[:, half:] = parts[0] - parts[1]
    for m in range(MODES):
        for a in range(8):
            tiles = [
                work[m * NZ + z * 8 : m * NZ + z * 8 + 8, 128 * a : 128 * a + 128]
                for z in range(ZP)
            ]
            for b in range(4):
                block = None
                for z in range(ZP):
                    shift = (32 * (z - b)) % 128
                    moved = tiles[z] if shift == 0 else pltpu.roll(tiles[z], shift, 1)
                    block = moved if block is None else jnp.where(lane == z, moved, block)
                out[pl.ds((4 * a + b) * 24 + m, 8, stride=3), :] = block


def gather_batches(origin_x, origin_z, planes, ya, atoms, grid, store):
    lane = iota((1, 128), 1)
    step_x = iota((XW, 128), 0).astype(F32)
    step_y = iota((24, 128), 0).astype(F32)
    step_z = iota((8, 128), 0).astype(F32)
    for batch in range(ATOMS // 128):
        own = slice(128 * batch, 128 * batch + 128)
        starts, base_y = y_blocks(ya, batch, lane)
        xs = (atoms[0:1, own] - origin_x) + 1.0
        ys = (atoms[1:2, own] - base_y) + 1.0
        zs = (atoms[2:3, own] - origin_z) + 1.0
        wx, sx = weights_of(step_x - xs)
        wy, sy = weights_of(step_y - ys)
        wz, sz = weights_of(step_z - zs)
        blocks = []
        level = jnp.zeros((1, 128), F32)
        for j in range(4):
            block = grid[pl.ds(starts[j], 3)].reshape(24, 128)
            middle = block[8:9, 44:45]
            level = jnp.where((lane >> 5) == j, middle, level)
            blocks.append((block - middle)[:, : XW * planes])
        b_high, b_low = split(jnp.concatenate(blocks, axis=0))
        y_both = jnp.concatenate([masked_blocks(wy, lane), masked_blocks(sy, lane)], axis=1)
        y_high, y_low = split(y_both)
        sampled = dot_tn(
            jnp.concatenate([b_high, b_low], axis=0), jnp.concatenate([y_high, y_high], axis=0)
        ) + dot_tn(b_high, y_low)
        along_x = along_y = along_z = jnp.zeros((XW, 128), F32)
        for z in range(planes):
            value = sampled[XW * z : XW * z + XW, :128]
            slope = sampled[XW * z : XW * z + XW, 128:]
            along_x = along_x + value * wz[z : z + 1]
            along_y = along_y + slope * wz[z : z + 1]
            along_z = along_z + value * sz[z : z + 1]
        minus = -atoms[3:4, own]
        kept = sz[0:1]
        for z in range(1, planes):
            kept = kept + sz[z : z + 1]
        store(
            own,
            minus * jnp.sum(along_x * sx, axis=0, keepdims=True),
            minus * jnp.sum(along_y * wx, axis=0, keepdims=True),
            minus * (jnp.sum(along_z * wx, axis=0, keepdims=True) + level * kept),
        )


def gather_rest_kernel(
    ya, atoms, held, even_high, even_low, even_fine, odd_high, odd_low, odd_fine, grid, out
):
    even = times_table(even_high[...], even_low[...], held[0 : NY // 2, :]) + dot(
        even_fine[...], finest(held[0:LOW_Y, :], 0)
    )
    odd = times_table(odd_high[...], odd_low[...], held[NY // 2 :, :]) + dot(
        odd_fine[...], finest(held[NY // 2 : NY // 2 + LOW_Y, :], 0)
    )
    grid[0:48] = (even + odd).reshape(48, 8, 128)
    grid[48:96] = (even - odd).reshape(48, 8, 128)
    grid[96:98] = grid[0:2]
    origin_x, origin_z = neighbour_origin()

    def store(own, fx, fy, fz):
        out[0:1, own] = fx
        out[1:2, own] = fy
        out[2:3, own] = fz

    gather_batches(origin_x, origin_z, ZP - 1, ya, atoms, grid, store)


def gather_own_kernel(ya, atoms, grid, near, halo, out):
    origin_x = (lax.axis_index("dom") * XD).astype(F32)
    origin_z = (lax.axis_index("pme") * ZP).astype(F32)

    def store(own, fx, fy, fz):
        forces = [fx, fy, fz]
        for f in range(3):
            total = forces[f] + near[f : f + 1, own]
            if own.start == 0:
                total = total + halo[f : f + 1, :]
            out[f : f + 1, own] = total

    gather_batches(origin_x, origin_z, ZP, ya, atoms, grid, store)


def pair_strength(dist_sq):
    inverse = lax.rsqrt(dist_sq)
    inverse = inverse * (1.5 - 0.5 * dist_sq * inverse * inverse)
    scaled = BETA * (dist_sq * inverse)
    t = 1.0 / (1.0 + 0.5 * scaled)
    poly = jnp.full_like(t, ERFC_Q[-1])
    for coefficient in ERFC_Q[-2::-1]:
        poly = poly * t + coefficient
    fall = jnp.exp(-(BETA * BETA) * dist_sq)
    bracket = t * poly * inverse + 2.0 * BETA / math.sqrt(math.pi)
    return fall * bracket * (inverse * inverse)


def nonbonded_kernel(atoms, turned, pairs, beyond, near, halo, weight, repeated, columns):
    left = pairs[0:1, :]
    right = pairs[1:2, :]
    inside = right < CLUSTERS
    cluster = iota((CLUSTERS, PAIRS), 0)
    hot_left = jnp.where(cluster == left, 1.0, 0.0).astype(BF16)
    hot_right = jnp.where(cluster == right, 1.0, 0.0).astype(BF16)
    code = iota((16, PAIRS), 0)
    code_left = jnp.where(
        code == jnp.where(inside, right & 3, right - (CLUSTERS - 4)), 1.0, 0.0
    ).astype(BF16)
    code_right = jnp.where(
        code == jnp.where(inside, left & 3, -1), 1.0, 0.0
    ).astype(BF16)
    count = dot_nt(code_left, hot_left) + dot_nt(code_right, hot_right)
    n_high, n_low = split(count)
    expand = jnp.where(
        (iota((CLUSTERS, ATOMS), 1) >> 3) == iota((CLUSTERS, ATOMS), 0), 1.0, 0.0
    ).astype(BF16)
    weight[...] = dot(n_high, expand) + dot(n_low, expand)
    turn_1 = turned[...].astype(BF16)
    rest = turned[...] - turn_1.astype(F32)
    turn_2 = rest.astype(BF16)
    turn_3 = (rest - turn_2.astype(F32)).astype(BF16)
    spreading = jnp.where(
        (iota((GROUPS, ATOMS), 1) >> 5) == iota((GROUPS, ATOMS), 0), 1.0, 0.0
    ).astype(BF16)
    repeated[...] = (dot(turn_1, spreading) + dot(turn_2, spreading)) + dot(turn_3, spreading)
    row = iota((8, 128), 0)
    lane = iota((8, 128), 1)
    for tile in range(ATOMS // 128):
        own = slice(128 * tile, 128 * tile + 128)
        px, py, pz = atoms[0:1, own], atoms[1:2, own], atoms[2:3, own]
        sum_x = sum_y = sum_z = jnp.zeros((8, 128), F32)
        for i in range(4):
            dx = px - repeated[8 * i : 8 * i + 8, own]
            dy = py - repeated[32 + 8 * i : 40 + 8 * i, own]
            dz = pz - repeated[64 + 8 * i : 72 + 8 * i, own]
            other = repeated[96 + 8 * i : 104 + 8 * i, own]
            dist_sq = (dx * dx + dy * dy) + dz * dz
            itself = (lane & 31) == (row + 8 * i)
            dist_sq = jnp.where(itself, 1.0, dist_sq)
            strength = pair_strength(dist_sq) * (other * weight[i : i + 1, own])
            sum_x = sum_x + strength * dx
            sum_y = sum_y + strength * dy
            sum_z = sum_z + strength * dz
        near[0:1, own] = jnp.sum(sum_x, axis=0, keepdims=True)
        near[1:2, own] = jnp.sum(sum_y, axis=0, keepdims=True)
        near[2:3, own] = jnp.sum(sum_z, axis=0, keepdims=True)
    lift = jnp.where(lax.axis_index("dom") == N_DOM - 1, float(NX), 0.0)
    upright = jnp.transpose(jnp.concatenate([beyond[...]] * 32, axis=0))
    columns[...] = jnp.zeros((128, 128), F32)
    for c in range(HALO_CLUSTERS):
        part = upright[8 * c : 8 * c + 8]
        hx = part[:, 0:1] + lift
        hy = part[:, 1:2]
        hz = part[:, 2:3]
        hq = part[:, 3:4]
        sum_x = sum_y = sum_z = jnp.zeros((8, 128), F32)
        for tile in range(ATOMS // 128):
            own = slice(128 * tile, 128 * tile + 128)
            dx = atoms[0:1, own] - hx
            dy = atoms[1:2, own] - hy
            dz = atoms[2:3, own] - hz
            dist_sq = (dx * dx + dy * dy) + dz * dz
            both = weight[4 + c : 5 + c, own]
            strength = pair_strength(dist_sq) * both
            on_own = strength * hq
            near[0:1, own] = near[0:1, own] + jnp.sum(on_own * dx, axis=0, keepdims=True)
            near[1:2, own] = near[1:2, own] + jnp.sum(on_own * dy, axis=0, keepdims=True)
            near[2:3, own] = near[2:3, own] + jnp.sum(on_own * dz, axis=0, keepdims=True)
            on_halo = strength * atoms[3:4, own]
            sum_x = sum_x - on_halo * dx
            sum_y = sum_y - on_halo * dy
            sum_z = sum_z - on_halo * dz
        force_x = jnp.sum(sum_x, axis=1, keepdims=True) * hq
        force_y = jnp.sum(sum_y, axis=1, keepdims=True) * hq
        force_z = jnp.sum(sum_z, axis=1, keepdims=True) * hq
        columns[8 * c : 8 * c + 8, :] = jnp.where(
            lane == 0, force_x, jnp.where(lane == 1, force_y, jnp.where(lane == 2, force_z, 0.0))
        )
    halo[...] = jnp.transpose(columns[...])[0:8]
    for f in range(3):
        near[f : f + 1, :] = near[f : f + 1, :] * atoms[3:4, 0:ATOMS]


def call(kernel, outs, ins, scratch=(), flops=1_000_000):
    vmem = pl.BlockSpec(memory_space=pltpu.VMEM)
    smem = pl.BlockSpec(memory_space=pltpu.SMEM)
    spaces = {"s": smem, "v": vmem, "h": pl.BlockSpec(memory_space=pltpu.HBM)}
    in_specs = [spaces[kind] for kind, _ in ins]
    many = isinstance(outs, list)
    return pl.pallas_call(
        kernel,
        out_shape=outs,
        in_specs=in_specs,
        out_specs=[vmem] * len(outs) if many else vmem,
        scratch_shapes=list(scratch),
        compiler_params=pltpu.CompilerParams(vmem_limit_bytes=VMEM_LIMIT),
        cost_estimate=pl.CostEstimate(flops=flops, bytes_accessed=1_000_000, transcendentals=0),
    )(*[x for _, x in ins])


def shape(*dims):
    return jax.ShapeDtypeStruct(dims, F32)


def permuted(x, axis, by):
    length = lax.axis_size(axis)
    return lax.ppermute(x, axis, [(i, (i + by) % length) for i in range(length)])


def exchange(x):
    sent = x.reshape(DEVICES, 1, MODES * 128)
    return lax.all_to_all(sent, ("dom", "pme"), 0, 0).reshape(DEVICES * MODES, 128)


def tables():
    along_y, y_waves = real_basis(NY)
    along_x, x_waves = real_basis(NX)
    along_z, z_waves = real_basis(NZ)
    folded = np.zeros((N_DOM * XW, NX))
    for q in range(N_DOM):
        for x in range(XD + 3):
            folded[q * XW + x] = along_x[:, (q * XD + x) % NX]
    order = np.array([4 * p + z for z in range(ZP) for p in range(N_PME)])
    z_rows = np.kron(np.eye(MODES), along_z[:, order])
    y_square, y_factor = wave_factors(y_waves, NY)
    y_info = np.zeros((DEVICES, 128))
    y_info[:, 0:MODES] = y_square.reshape(DEVICES, MODES)
    y_info[:, MODES : 2 * MODES] = y_factor.reshape(DEVICES, MODES)
    x_square, x_factor = wave_factors(x_waves, NX)
    z_square, z_factor = wave_factors(z_waves, NZ)
    f32 = np.float32

    def back(table, low):
        return (*halves(table), thirds(table[:, :low], 1))

    return {
        "y_even": halves(along_y[: NY // 2, : NY // 2]),
        "y_odd": halves(along_y[NY // 2 :, : NY // 2]),
        "y_even_back": back(along_y[: NY // 2, : NY // 2].T, LOW_Y),
        "y_odd_back": back(along_y[NY // 2 :, : NY // 2].T, LOW_Y),
        "x_even": back(folded[: N_DOM // 2 * XW, : NX // 2], LOW_X),
        "x_odd": back(folded[: N_DOM // 2 * XW, NX // 2 :], LOW_X),
        "z": halves(z_rows),
        "z_back": back(z_rows.T, MODES * NZ),
        "y_info": y_info.astype(f32),
        "x_square": x_square.astype(f32)[None, :],
        "x_factor": (x_factor / math.pi).astype(f32)[None, :],
        "z_square": np.repeat(z_square.astype(f32)[:, None], 128, axis=1),
        "z_factor": np.repeat(z_factor.astype(f32)[:, None], 128, axis=1),
    }


def make_shards(table):
    def shards(group_column, group_corner, atom_cell, fraction, charge, cluster_pairs):
        column = group_column.reshape(1, GROUPS)
        atoms, edge = call(
            prepare_kernel,
            [shape(4, CARRIED), shape(4, 128)],
            [
                ("h", pltpu.with_memory_space_constraint(column, pltpu.HBM)),
                ("h", pltpu.with_memory_space_constraint(group_corner, pltpu.HBM)),
                ("h", pltpu.with_memory_space_constraint(atom_cell, pltpu.HBM)),
                ("h", pltpu.with_memory_space_constraint(fraction, pltpu.HBM)),
                ("h", pltpu.with_memory_space_constraint(charge.reshape(1, ATOMS), pltpu.HBM)),
            ],
            scratch=[
                pltpu.VMEM((1, GROUPS), jnp.int32),
                pltpu.VMEM((3, GROUPS), jnp.int32),
                pltpu.VMEM((3, ATOMS), jnp.int32),
                pltpu.VMEM((3, ATOMS), F32),
                pltpu.VMEM((1, ATOMS), F32),
                pltpu.SemaphoreType.DMA((5,)),
            ],
        )
        behind = permuted(atoms, "pme", 1)
        beyond = permuted(edge, "dom", -1)
        ya = (column[0] * YP + group_corner[1]) >> 3
        own_grid = call(
            spread_own_kernel,
            shape(BLOCKS, 8, 128),
            [("s", ya), ("v", atoms)],
            flops=3_000_000_000,
        )
        ya_behind = behind[0, ATOMS : ATOMS + GROUPS].astype(jnp.int32) >> 3
        spectrum = call(
            spread_rest_kernel,
            shape(NY, 128),
            [
                ("s", ya_behind), ("v", behind), ("v", own_grid),
                *[("v", x) for x in table["y_even"] + table["y_odd"]],
            ],
            scratch=[pltpu.VMEM((BLOCKS, 8, 128), F32)],
        )
        held = exchange(spectrum)
        turned = atoms[:, :ATOMS].reshape(4, GROUPS, 32).transpose(0, 2, 1).reshape(128, GROUPS)
        near, halo = call(
            nonbonded_kernel,
            [shape(3, ATOMS), shape(8, 128)],
            [("v", atoms), ("v", turned), ("v", cluster_pairs), ("v", beyond)],
            scratch=[
                pltpu.VMEM((16, ATOMS), F32),
                pltpu.VMEM((128, ATOMS), F32),
                pltpu.VMEM((128, 128), F32),
            ],
            flops=8_000_000_000,
        )
        halo_back = permuted(halo, "dom", 1)
        filtered = call(
            filter_kernel,
            shape(DEVICES * MODES, 128),
            [
                ("v", table["y_info"]), ("v", held),
                *[("v", x) for x in table["x_even"][:2] + table["x_odd"][:2]],
                ("v", table["x_even"][2]), ("v", table["x_odd"][2]),
                *[("v", x) for x in table["z"] + table["z_back"]],
                ("v", table["x_square"]), ("v", table["x_factor"]),
                ("v", table["z_square"]), ("v", table["z_factor"]),
            ],
            scratch=[pltpu.VMEM((MODES * NZ, N_DOM * XW), F32)],
        )
        returned = exchange(filtered)
        grid, rest = call(
            gather_rest_kernel,
            [shape(BLOCKS, 8, 128), shape(3, ATOMS)],
            [
                ("s", ya_behind), ("v", behind), ("v", returned),
                *[("v", x) for x in table["y_even_back"] + table["y_odd_back"]],
            ],
        )
        rest_back = permuted(rest, "pme", -1)
        forces = call(
            gather_own_kernel,
            shape(3, ATOMS),
            [
                ("s", ya), ("v", atoms), ("v", grid), ("v", near),
                ("v", halo_back),
            ],
            flops=3_000_000_000,
        )
        return forces + rest_back

    return shards


def solution(mesh):
    in_specs = (
        P(("pme", "dom"), None),
        P(None, ("pme", "dom")),
        P(None, ("pme", "dom")),
        P(None, ("pme", "dom")),
        P(("pme", "dom")),
        P(None, ("pme", "dom")),
    )
    out_specs = P(None, ("pme", "dom"))
    return jax.shard_map(
        make_shards(tables()), mesh=mesh, in_specs=in_specs, out_specs=out_specs, check_vma=False
    )
```

```python
import math

import jax
import jax.numpy as jnp
import ml_dtypes
import numpy as np
from jax import lax
from jax.experimental import pallas as pl
from jax.experimental.pallas import tpu as pltpu
from jax.sharding import PartitionSpec as P

NX = 768
NY = 768
NZ = 32
N_DOM = 32
N_PME = 8
DEVICES = 256
XD = 24
YP = 24
ZP = 4
GROUPS = 64
ATOMS = 2048
CARRIED = ATOMS + 128
PAIRS = 1024
CLUSTERS = 256
HALO_CLUSTERS = 8
HALO_ATOMS = 64
XW = 32
MODES = 3
LOW_Y = 64
LOW_X = 128
ROWS = NY + 16
SPAN = 16
BETA = 0.35
VMEM_LIMIT = 24 * 1024 * 1024

F32 = jnp.float32
BF16 = jnp.bfloat16

ERFC_Q = (
    0.2820947951,
    0.2820937768,
    0.2468838798,
    0.1753240754,
    0.0934147485,
    -0.05905091002,
    0.1318500403,
    -0.4545637183,
    0.493385742,
    -0.2346054907,
    0.04317306594,
)


def real_basis(length):
    point = np.arange(length)
    rows = np.zeros((length, length))
    waves = np.zeros(length, np.int64)
    rows[0] = 1.0 / math.sqrt(length)
    for k in range(1, length // 2):
        angle = 2.0 * math.pi * (k * point % length) / length
        rows[2 * k - 1] = math.sqrt(2.0 / length) * np.cos(angle)
        rows[2 * k] = math.sqrt(2.0 / length) * np.sin(angle)
        waves[2 * k - 1] = k
        waves[2 * k] = k
    rows[length - 1] = (1.0 - 2.0 * (point % 2)) / math.sqrt(length)
    waves[length - 1] = length // 2
    order = np.argsort(waves % 2, kind="stable")
    return rows[order], waves[order]


def wave_factors(waves, length):
    freq = waves / length
    modulus = 1.0 / (2.0 / 3.0 + np.cos(2.0 * math.pi * waves / length) / 3.0) ** 2
    return freq * freq, np.exp(-((math.pi / BETA) ** 2) * freq * freq) * modulus


def halves(table):
    table = table.astype(np.float32)
    high = table.astype(ml_dtypes.bfloat16)
    low = (table - high.astype(np.float32)).astype(ml_dtypes.bfloat16)
    return high, low


def thirds(table, axis):
    table = table.astype(np.float32)
    high, middle = halves(table)
    low = (table - high.astype(np.float32)) - middle.astype(np.float32)
    return np.concatenate([low.astype(ml_dtypes.bfloat16), high, middle], axis=axis)


def finest(value, axis):
    high = value.astype(BF16)
    rest = value - high.astype(F32)
    middle = rest.astype(BF16)
    low = (rest - middle.astype(F32)).astype(BF16)
    return jnp.concatenate([high, low, middle], axis=axis)


def split(value):
    high = value.astype(BF16)
    low = (value - high.astype(F32)).astype(BF16)
    return high, low


def dot(a, b):
    return jnp.dot(a, b, preferred_element_type=F32)


def dot_nt(a, b):
    return lax.dot_general(a, b, (((1,), (1,)), ((), ())), preferred_element_type=F32)


def dot_tn(a, b):
    return lax.dot_general(a, b, (((0,), (0,)), ((), ())), preferred_element_type=F32)


def times_table(table_high, table_low, value):
    high, low = split(value)
    both = dot(table_high, jnp.concatenate([high, low], axis=1))
    return both[:, :128] + (both[:, 128:] + dot(table_low, high))


def iota(shape, dim):
    return lax.broadcasted_iota(jnp.int32, shape, dim)


def spline(u):
    d = jnp.abs(u)
    a = jnp.maximum(2.0 - d, 0.0)
    b = jnp.maximum(1.0 - d, 0.0)
    return (a * a * a - 4.0 * (b * b * b)) * (1.0 / 6.0)


def spline_slope(u):
    d = jnp.abs(u)
    a = jnp.maximum(2.0 - d, 0.0)
    b = jnp.maximum(1.0 - d, 0.0)
    slope = 0.5 * (a * a) - 2.0 * (b * b)
    return slope, (a * a * a - 4.0 * (b * b * b)) * (1.0 / 6.0)


def weights_of(u):
    slope, value = spline_slope(u)
    return value, jnp.where(u < 0.0, -slope, slope)


def prepare_kernel(
    col_in, corner_in, cell_in, fraction_in, charge_in, atoms, edge,
    col, corner, cell, fraction, charge, arrived,
):
    copies = [
        pltpu.make_async_copy(source, target, arrived.at[i])
        for i, (source, target) in enumerate(
            (
                (col_in, col), (corner_in, corner), (cell_in, cell),
                (fraction_in, fraction), (charge_in, charge),
            )
        )
    ]
    for copy in copies:
        copy.start()
    for copy in copies:
        copy.wait()
    group = iota((GROUPS, ATOMS), 0)
    hot = jnp.where((iota((GROUPS, ATOMS), 1) >> 5) == group, 1.0, 0.0).astype(BF16)
    rep_corner = dot(corner[...].astype(F32).astype(BF16), hot)
    rep_col = dot(
        jnp.broadcast_to(col[...].astype(F32), (8, GROUPS)).astype(BF16), hot
    )[0:1]
    base = rep_corner + cell[...].astype(F32)
    first = (lax.axis_index("dom") * XD).astype(F32)
    third = (lax.axis_index("pme") * ZP).astype(F32)
    along_x = (base[0:1] + first) + fraction[0:1, :]
    along_y = (base[1:2] + rep_col * float(YP)) + fraction[1:2, :]
    along_z = (base[2:3] + third) + fraction[2:3, :]
    atoms[0:1, 0:ATOMS] = along_x
    atoms[1:2, 0:ATOMS] = along_y
    atoms[2:3, 0:ATOMS] = along_z
    atoms[3:4, 0:ATOMS] = charge[...]
    atoms[:, ATOMS:] = jnp.zeros((4, 128), F32)
    lowest = (col[...] * YP + corner[1:2, :]).astype(F32)
    atoms[0:1, ATOMS : ATOMS + GROUPS] = lowest
    edge[...] = atoms[:, 0:128]


def y_starts(ya, batch, lane):
    starts = [ya[4 * batch + j] for j in range(4)]
    row = jnp.where(
        lane < 64,
        jnp.where(lane < 32, starts[0], starts[1]),
        jnp.where(lane < 96, starts[2], starts[3]),
    )
    return starts, row.astype(F32)


def masked_blocks(weights, lane):
    return jnp.concatenate(
        [jnp.where((lane >> 5) == j, weights, 0.0) for j in range(4)], axis=0
    )


def spread_batches(origin_x, origin_z, planes, ya, atoms, grid):
    lane = iota((1, 128), 1)
    step_x = iota((XW, 128), 0).astype(F32)
    step_y = iota((SPAN, 128), 0).astype(F32)
    step_z = iota((8, 128), 0).astype(F32)
    for batch in range(ATOMS // 128):
        own = slice(128 * batch, 128 * batch + 128)
        starts, base_y = y_starts(ya, batch, lane)
        xs = (atoms[0:1, own] - origin_x) + 1.0
        ys = (atoms[1:2, own] - base_y) + 1.0
        zs = (atoms[2:3, own] - origin_z) + 1.0
        wx = spline(step_x - xs)
        wz = spline(step_z - zs) * atoms[3:4, own]
        wy = masked_blocks(spline(step_y - ys), lane)
        charged = jnp.concatenate([wx * wz[z : z + 1] for z in range(planes)], axis=0)
        c_high, c_low = split(charged)
        y_high, y_low = split(wy)
        added = dot_nt(
            jnp.concatenate([y_high, y_low], axis=1), jnp.concatenate([c_high, c_high], axis=1)
        ) + dot_nt(y_high, c_low)
        for j in range(4):
            where = (pl.ds(starts[j], SPAN), slice(0, XW * planes))
            grid[where] = grid[where] + added[SPAN * j : SPAN * j + SPAN]


def spread_own_kernel(ya, atoms, grid):
    grid[...] = jnp.zeros((ROWS, 128), F32)
    origin_x = (lax.axis_index("dom") * XD).astype(F32)
    origin_z = (lax.axis_index("pme") * ZP).astype(F32)
    spread_batches(origin_x, origin_z, ZP, ya, atoms, grid)


def neighbour_origin():
    behind = (lax.axis_index("pme") + (N_PME - 1)) & (N_PME - 1)
    return (lax.axis_index("dom") * XD).astype(F32), (behind * ZP + ZP).astype(F32)


def spread_rest_kernel(ya, atoms, own, even_high, even_low, odd_high, odd_low, out, grid):
    grid[...] = own[...]
    origin_x, origin_z = neighbour_origin()
    spread_batches(origin_x, origin_z, ZP - 1, ya, atoms, grid)
    grid[0:16, :] = grid[0:16, :] + grid[NY:ROWS, :]
    lower = grid[0 : NY // 2, :]
    upper = grid[NY // 2 : NY, :]
    out[0 : NY // 2, :] = times_table(even_high[...], even_low[...], lower + upper)
    out[NY // 2 :, :] = times_table(odd_high[...], odd_low[...], lower - upper)


def filter_kernel(
    y_info, held, even_high, even_low, odd_high, odd_low, even_fine, odd_fine, kz_high, kz_low, tz_high, tz_low, tz_fine,
    x_square, x_factor, z_square, z_factor, out, work,
):
    lane = iota((8, 128), 1) >> 5
    for m in range(MODES):
        for a in range(8):
            blocks = [
                held[pl.ds((4 * a + b) * MODES + m, 8, stride=N_DOM * MODES), :] for b in range(4)
            ]
            for z in range(ZP):
                tile = None
                for b in range(4):
                    shift = (32 * (b - z)) % 128
                    moved = blocks[b] if shift == 0 else pltpu.roll(blocks[b], shift, 1)
                    tile = moved if tile is None else jnp.where(lane == b, moved, tile)
                row = m * NZ + z * 8
                work[row : row + 8, 128 * a : 128 * a + 128] = tile
    rows = MODES * NZ
    half = N_DOM // 2 * XW
    lower, upper = work[:, :half], work[:, half:]
    waves = []
    for value, high, low in ((lower + upper, even_high, even_low), (lower - upper, odd_high, odd_low)):
        v_high, v_low = split(value)
        both = dot(jnp.concatenate([v_high, v_low], axis=0), high[...])
        waves.append(both[:rows] + (both[rows:] + dot(v_high, low[...])))
    w_high, w_low = split(jnp.concatenate(waves, axis=1))
    full = dot(kz_high[...], w_high) + (dot(kz_high[...], w_low) + dot(kz_low[...], w_high))
    device = lax.axis_index("pme") * N_DOM + lax.axis_index("dom")
    info = y_info[pl.ds(device, 1), :]
    scaled = []
    for m in range(MODES):
        square = (x_square[...] + z_square[:, 0:1]) + info[:, m : m + 1]
        factor = (x_factor[...] * z_factor[:, 0:1]) * info[:, MODES + m : MODES + m + 1]
        nonzero = jnp.where(square > 0.0, square, 1.0)
        influence = jnp.where(square > 0.0, factor / nonzero, 0.0)
        scaled.append(full[m * NZ : m * NZ + NZ] * influence)
    scaled = jnp.concatenate(scaled, axis=0)
    s_high, s_low = split(scaled)
    back = dot(tz_high[...], s_high) + (
        dot(tz_high[...], s_low)
        + (dot(tz_low[...], s_high) + dot(tz_fine[...], finest(scaled, 0)))
    )
    parts = []
    for value, high, low, fine in (
        (back[:, : NX // 2], even_high, even_low, even_fine),
        (back[:, NX // 2 :], odd_high, odd_low, odd_fine),
    ):
        v_high, v_low = split(value)
        both = dot_nt(jnp.concatenate([v_high, v_low], axis=0), high[...])
        small = dot_nt(v_high, low[...]) + dot_nt(finest(value[:, :LOW_X], 1), fine[...])
        parts.append(both[:rows] + (both[rows:] + small))
    work[:, :half] = parts[0] + parts[1]
    work[:, half:] = parts[0] - parts[1]
    for m in range(MODES):
        for a in range(8):
            tiles = [
                work[m * NZ + z * 8 : m * NZ + z * 8 + 8, 128 * a : 128 * a + 128]
                for z in range(ZP)
            ]
            for b in range(4):
                block = None
                for z in range(ZP):
                    shift = (32 * (z - b)) % 128
                    moved = tiles[z] if shift == 0 else pltpu.roll(tiles[z], shift, 1)
                    block = moved if block is None else jnp.where(lane == z, moved, block)
                out[pl.ds((4 * a + b) * MODES + m, 8, stride=N_DOM * MODES), :] = block


def gather_batches(origin_x, origin_z, planes, ya, atoms, grid, store):
    lane = iota((1, 128), 1)
    step_x = iota((XW, 128), 0).astype(F32)
    step_y = iota((SPAN, 128), 0).astype(F32)
    step_z = iota((8, 128), 0).astype(F32)
    for batch in range(ATOMS // 128):
        own = slice(128 * batch, 128 * batch + 128)
        starts, base_y = y_starts(ya, batch, lane)
        xs = (atoms[0:1, own] - origin_x) + 1.0
        ys = (atoms[1:2, own] - base_y) + 1.0
        zs = (atoms[2:3, own] - origin_z) + 1.0
        wx, sx = weights_of(step_x - xs)
        wy, sy = weights_of(step_y - ys)
        wz, sz = weights_of(step_z - zs)
        blocks = []
        level = jnp.zeros((1, 128), F32)
        for j in range(4):
            block = grid[pl.ds(starts[j], SPAN), :]
            middle = block[8:9, 44:45]
            level = jnp.where((lane >> 5) == j, middle, level)
            blocks.append((block - middle)[:, : XW * planes])
        b_high, b_low = split(jnp.concatenate(blocks, axis=0))
        y_both = jnp.concatenate([masked_blocks(wy, lane), masked_blocks(sy, lane)], axis=1)
        y_high, y_low = split(y_both)
        sampled = dot_tn(
            jnp.concatenate([b_high, b_low, b_high], axis=0),
            jnp.concatenate([y_high, y_high, y_low], axis=0),
        )
        along_x = along_y = along_z = jnp.zeros((XW, 128), F32)
        for z in range(planes):
            value = sampled[XW * z : XW * z + XW, :128]
            slope = sampled[XW * z : XW * z + XW, 128:]
            along_x = along_x + value * wz[z : z + 1]
            along_y = along_y + slope * wz[z : z + 1]
            along_z = along_z + value * sz[z : z + 1]
        minus = -atoms[3:4, own]
        kept = sz[0:1]
        for z in range(1, planes):
            kept = kept + sz[z : z + 1]
        store(
            own,
            minus * jnp.sum(along_x * sx, axis=0, keepdims=True),
            minus * jnp.sum(along_y * wx, axis=0, keepdims=True),
            minus * (jnp.sum(along_z * wx, axis=0, keepdims=True) + level * kept),
        )


def gather_rest_kernel(
    ya, atoms, held, even_high, even_low, even_fine, odd_high, odd_low, odd_fine, grid, out
):
    even = times_table(even_high[...], even_low[...], held[0 : NY // 2, :]) + dot(
        even_fine[...], finest(held[0:LOW_Y, :], 0)
    )
    odd = times_table(odd_high[...], odd_low[...], held[NY // 2 :, :]) + dot(
        odd_fine[...], finest(held[NY // 2 : NY // 2 + LOW_Y, :], 0)
    )
    grid[0 : NY // 2, :] = even + odd
    grid[NY // 2 : NY, :] = even - odd
    grid[NY:ROWS, :] = (even + odd)[0:16]
    origin_x, origin_z = neighbour_origin()

    def store(own, fx, fy, fz):
        out[0:1, own] = fx
        out[1:2, own] = fy
        out[2:3, own] = fz

    gather_batches(origin_x, origin_z, ZP - 1, ya, atoms, grid, store)


def gather_own_kernel(ya, atoms, grid, near, halo, out):
    origin_x = (lax.axis_index("dom") * XD).astype(F32)
    origin_z = (lax.axis_index("pme") * ZP).astype(F32)

    def store(own, fx, fy, fz):
        forces = [fx, fy, fz]
        for f in range(3):
            total = forces[f] + near[f : f + 1, own]
            if own.start == 0:
                total = total + halo[f : f + 1, :]
            out[f : f + 1, own] = total

    gather_batches(origin_x, origin_z, ZP, ya, atoms, grid, store)


def pair_strength(dist_sq):
    inverse = lax.rsqrt(dist_sq)
    inverse = inverse * (1.5 - 0.5 * dist_sq * inverse * inverse)
    scaled = BETA * (dist_sq * inverse)
    t = 1.0 / (1.0 + 0.5 * scaled)
    poly = jnp.full_like(t, ERFC_Q[-1])
    for coefficient in ERFC_Q[-2::-1]:
        poly = poly * t + coefficient
    fall = jnp.exp(-(BETA * BETA) * dist_sq)
    bracket = t * poly * inverse + 2.0 * BETA / math.sqrt(math.pi)
    return fall * bracket * (inverse * inverse)


def nonbonded_kernel(atoms, turned, pairs, beyond, near, halo, weight, repeated, columns):
    left = pairs[0:1, :]
    right = pairs[1:2, :]
    inside = right < CLUSTERS
    cluster = iota((CLUSTERS, PAIRS), 0)
    hot_left = jnp.where(cluster == left, 1.0, 0.0).astype(BF16)
    hot_right = jnp.where(cluster == right, 1.0, 0.0).astype(BF16)
    code = iota((16, PAIRS), 0)
    code_left = jnp.where(
        code == jnp.where(inside, right & 3, right - (CLUSTERS - 4)), 1.0, 0.0
    ).astype(BF16)
    code_right = jnp.where(
        code == jnp.where(inside, left & 3, -1), 1.0, 0.0
    ).astype(BF16)
    count = dot_nt(code_left, hot_left) + dot_nt(code_right, hot_right)
    n_high, n_low = split(count)
    expand = jnp.where(
        (iota((CLUSTERS, ATOMS), 1) >> 3) == iota((CLUSTERS, ATOMS), 0), 1.0, 0.0
    ).astype(BF16)
    weight[...] = dot(n_high, expand) + dot(n_low, expand)
    turn_1 = turned[...].astype(BF16)
    rest = turned[...] - turn_1.astype(F32)
    turn_2 = rest.astype(BF16)
    turn_3 = (rest - turn_2.astype(F32)).astype(BF16)
    spreading = jnp.where(
        (iota((GROUPS, ATOMS), 1) >> 5) == iota((GROUPS, ATOMS), 0), 1.0, 0.0
    ).astype(BF16)
    repeated[...] = (dot(turn_1, spreading) + dot(turn_2, spreading)) + dot(turn_3, spreading)
    row = iota((8, 128), 0)
    lane = iota((8, 128), 1)
    for tile in range(ATOMS // 128):
        own = slice(128 * tile, 128 * tile + 128)
        px, py, pz = atoms[0:1, own], atoms[1:2, own], atoms[2:3, own]
        sum_x = sum_y = sum_z = jnp.zeros((8, 128), F32)
        for i in range(4):
            dx = px - repeated[8 * i : 8 * i + 8, own]
            dy = py - repeated[32 + 8 * i : 40 + 8 * i, own]
            dz = pz - repeated[64 + 8 * i : 72 + 8 * i, own]
            other = repeated[96 + 8 * i : 104 + 8 * i, own]
            dist_sq = (dx * dx + dy * dy) + dz * dz
            itself = (lane & 31) == (row + 8 * i)
            dist_sq = jnp.where(itself, 1.0, dist_sq)
            strength = pair_strength(dist_sq) * (other * weight[i : i + 1, own])
            sum_x = sum_x + strength * dx
            sum_y = sum_y + strength * dy
            sum_z = sum_z + strength * dz
        near[0:1, own] = jnp.sum(sum_x, axis=0, keepdims=True)
        near[1:2, own] = jnp.sum(sum_y, axis=0, keepdims=True)
        near[2:3, own] = jnp.sum(sum_z, axis=0, keepdims=True)
    lift = jnp.where(lax.axis_index("dom") == N_DOM - 1, float(NX), 0.0)
    upright = jnp.transpose(jnp.concatenate([beyond[...]] * 32, axis=0))
    columns[...] = jnp.zeros((128, 128), F32)
    for c in range(HALO_CLUSTERS):
        part = upright[8 * c : 8 * c + 8]
        hx = part[:, 0:1] + lift
        hy = part[:, 1:2]
        hz = part[:, 2:3]
        hq = part[:, 3:4]
        sum_x = sum_y = sum_z = jnp.zeros((8, 128), F32)
        for tile in range(ATOMS // 128):
            own = slice(128 * tile, 128 * tile + 128)
            dx = atoms[0:1, own] - hx
            dy = atoms[1:2, own] - hy
            dz = atoms[2:3, own] - hz
            dist_sq = (dx * dx + dy * dy) + dz * dz
            both = weight[4 + c : 5 + c, own]
            strength = pair_strength(dist_sq) * both
            on_own = strength * hq
            near[0:1, own] = near[0:1, own] + jnp.sum(on_own * dx, axis=0, keepdims=True)
            near[1:2, own] = near[1:2, own] + jnp.sum(on_own * dy, axis=0, keepdims=True)
            near[2:3, own] = near[2:3, own] + jnp.sum(on_own * dz, axis=0, keepdims=True)
            on_halo = strength * atoms[3:4, own]
            sum_x = sum_x - on_halo * dx
            sum_y = sum_y - on_halo * dy
            sum_z = sum_z - on_halo * dz
        force_x = jnp.sum(sum_x, axis=1, keepdims=True) * hq
        force_y = jnp.sum(sum_y, axis=1, keepdims=True) * hq
        force_z = jnp.sum(sum_z, axis=1, keepdims=True) * hq
        columns[8 * c : 8 * c + 8, :] = jnp.where(
            lane == 0, force_x, jnp.where(lane == 1, force_y, jnp.where(lane == 2, force_z, 0.0))
        )
    halo[...] = jnp.transpose(columns[...])[0:8]
    for f in range(3):
        near[f : f + 1, :] = near[f : f + 1, :] * atoms[3:4, 0:ATOMS]


def call(kernel, outs, ins, scratch=(), flops=1_000_000):
    vmem = pl.BlockSpec(memory_space=pltpu.VMEM)
    smem = pl.BlockSpec(memory_space=pltpu.SMEM)
    spaces = {"s": smem, "v": vmem, "h": pl.BlockSpec(memory_space=pltpu.HBM)}
    in_specs = [spaces[kind] for kind, _ in ins]
    many = isinstance(outs, list)
    return pl.pallas_call(
        kernel,
        out_shape=outs,
        in_specs=in_specs,
        out_specs=[vmem] * len(outs) if many else vmem,
        scratch_shapes=list(scratch),
        compiler_params=pltpu.CompilerParams(vmem_limit_bytes=VMEM_LIMIT),
        cost_estimate=pl.CostEstimate(flops=flops, bytes_accessed=1_000_000, transcendentals=0),
    )(*[x for _, x in ins])


def shape(*dims):
    return jax.ShapeDtypeStruct(dims, F32)


def permuted(x, axis, by):
    length = lax.axis_size(axis)
    return lax.ppermute(x, axis, [(i, (i + by) % length) for i in range(length)])


def exchange(x):
    sent = x.reshape(DEVICES, 1, MODES * 128)
    return lax.all_to_all(sent, ("pme", "dom"), 0, 0).reshape(DEVICES * MODES, 128)


def tables():
    along_y, y_waves = real_basis(NY)
    along_x, x_waves = real_basis(NX)
    along_z, z_waves = real_basis(NZ)
    folded = np.zeros((N_DOM * XW, NX))
    for q in range(N_DOM):
        for x in range(XD + 3):
            folded[q * XW + x] = along_x[:, (q * XD + x) % NX]
    order = np.array([4 * p + z for z in range(ZP) for p in range(N_PME)])
    z_rows = np.kron(np.eye(MODES), along_z[:, order])
    y_square, y_factor = wave_factors(y_waves, NY)
    y_info = np.zeros((DEVICES, 128))
    y_info[:, 0:MODES] = y_square.reshape(DEVICES, MODES)
    y_info[:, MODES : 2 * MODES] = y_factor.reshape(DEVICES, MODES)
    x_square, x_factor = wave_factors(x_waves, NX)
    z_square, z_factor = wave_factors(z_waves, NZ)
    f32 = np.float32

    def back(table, low):
        return (*halves(table), thirds(table[:, :low], 1))

    return {
        "y_even": halves(along_y[: NY // 2, : NY // 2]),
        "y_odd": halves(along_y[NY // 2 :, : NY // 2]),
        "y_even_back": back(along_y[: NY // 2, : NY // 2].T, LOW_Y),
        "y_odd_back": back(along_y[NY // 2 :, : NY // 2].T, LOW_Y),
        "x_even": back(folded[: N_DOM // 2 * XW, : NX // 2], LOW_X),
        "x_odd": back(folded[: N_DOM // 2 * XW, NX // 2 :], LOW_X),
        "z": halves(z_rows),
        "z_back": back(z_rows.T, MODES * NZ),
        "y_info": y_info.astype(f32),
        "x_square": x_square.astype(f32)[None, :],
        "x_factor": (x_factor / math.pi).astype(f32)[None, :],
        "z_square": np.repeat(z_square.astype(f32)[:, None], 128, axis=1),
        "z_factor": np.repeat(z_factor.astype(f32)[:, None], 128, axis=1),
    }


def make_shards(table):
    def shards(group_column, group_corner, atom_cell, fraction, charge, cluster_pairs):
        column = group_column.reshape(1, GROUPS)
        atoms, edge = call(
            prepare_kernel,
            [shape(4, CARRIED), shape(4, 128)],
            [
                ("h", pltpu.with_memory_space_constraint(column, pltpu.HBM)),
                ("h", pltpu.with_memory_space_constraint(group_corner, pltpu.HBM)),
                ("h", pltpu.with_memory_space_constraint(atom_cell, pltpu.HBM)),
                ("h", pltpu.with_memory_space_constraint(fraction, pltpu.HBM)),
                ("h", pltpu.with_memory_space_constraint(charge.reshape(1, ATOMS), pltpu.HBM)),
            ],
            scratch=[
                pltpu.VMEM((1, GROUPS), jnp.int32),
                pltpu.VMEM((3, GROUPS), jnp.int32),
                pltpu.VMEM((3, ATOMS), jnp.int32),
                pltpu.VMEM((3, ATOMS), F32),
                pltpu.VMEM((1, ATOMS), F32),
                pltpu.SemaphoreType.DMA((5,)),
            ],
        )
        behind = permuted(atoms, "pme", 1)
        beyond = permuted(edge, "dom", -1)
        ya = column[0] * YP + group_corner[1]
        own_grid = call(
            spread_own_kernel,
            shape(ROWS, 128),
            [("s", ya), ("v", atoms)],
            flops=3_000_000_000,
        )
        ya_behind = behind[0, ATOMS : ATOMS + GROUPS].astype(jnp.int32)
        spectrum = call(
            spread_rest_kernel,
            shape(NY, 128),
            [
                ("s", ya_behind), ("v", behind), ("v", own_grid),
                *[("v", x) for x in table["y_even"] + table["y_odd"]],
            ],
            scratch=[pltpu.VMEM((ROWS, 128), F32)],
        )
        held = exchange(spectrum)
        turned = atoms[:, :ATOMS].reshape(4, GROUPS, 32).transpose(0, 2, 1).reshape(128, GROUPS)
        near, halo = call(
            nonbonded_kernel,
            [shape(3, ATOMS), shape(8, 128)],
            [("v", atoms), ("v", turned), ("v", cluster_pairs), ("v", beyond)],
            scratch=[
                pltpu.VMEM((16, ATOMS), F32),
                pltpu.VMEM((128, ATOMS), F32),
                pltpu.VMEM((128, 128), F32),
            ],
            flops=8_000_000_000,
        )
        halo_back = permuted(halo, "dom", 1)
        filtered = call(
            filter_kernel,
            shape(DEVICES * MODES, 128),
            [
                ("v", table["y_info"]), ("v", held),
                *[("v", x) for x in table["x_even"][:2] + table["x_odd"][:2]],
                ("v", table["x_even"][2]), ("v", table["x_odd"][2]),
                *[("v", x) for x in table["z"] + table["z_back"]],
                ("v", table["x_square"]), ("v", table["x_factor"]),
                ("v", table["z_square"]), ("v", table["z_factor"]),
            ],
            scratch=[pltpu.VMEM((MODES * NZ, N_DOM * XW), F32)],
        )
        returned = exchange(filtered)
        grid, rest = call(
            gather_rest_kernel,
            [shape(ROWS, 128), shape(3, ATOMS)],
            [
                ("s", ya_behind), ("v", behind), ("v", returned),
                *[("v", x) for x in table["y_even_back"] + table["y_odd_back"]],
            ],
        )
        rest_back = permuted(rest, "pme", -1)
        forces = call(
            gather_own_kernel,
            shape(3, ATOMS),
            [
                ("s", ya), ("v", atoms), ("v", grid), ("v", near),
                ("v", halo_back),
            ],
            flops=3_000_000_000,
        )
        return forces + rest_back

    return shards


def solution(mesh):
    in_specs = (
        P(("pme", "dom"), None),
        P(None, ("pme", "dom")),
        P(None, ("pme", "dom")),
        P(None, ("pme", "dom")),
        P(("pme", "dom")),
        P(None, ("pme", "dom")),
    )
    out_specs = P(None, ("pme", "dom"))
    return jax.shard_map(
        make_shards(tables()), mesh=mesh, in_specs=in_specs, out_specs=out_specs, check_vma=False
    )
```

```python
import math

import jax
import jax.numpy as jnp
import ml_dtypes
import numpy as np
from jax import lax
from jax.experimental import pallas as pl
from jax.experimental.pallas import tpu as pltpu
from jax.sharding import PartitionSpec as P

NX = 768
NY = 768
NZ = 32
N_DOM = 32
N_PME = 8
DEVICES = 256
XD = 24
YP = 24
ZP = 4
GROUPS = 64
ATOMS = 2048
CARRIED = ATOMS + 128
PAIRS = 1024
CLUSTERS = 256
HALO_CLUSTERS = 8
HALO_ATOMS = 64
XW = 32
MODES = 3
LOW_Y = 64
LOW_X = 128
ROWS = NY + 16
SPAN = 16
BETA = 0.35
VMEM_LIMIT = 24 * 1024 * 1024

F32 = jnp.float32
BF16 = jnp.bfloat16

ERFC_Q = (
    0.2820947951,
    0.2820937768,
    0.2468838798,
    0.1753240754,
    0.0934147485,
    -0.05905091002,
    0.1318500403,
    -0.4545637183,
    0.493385742,
    -0.2346054907,
    0.04317306594,
)


def real_basis(length):
    point = np.arange(length)
    rows = np.zeros((length, length))
    waves = np.zeros(length, np.int64)
    rows[0] = 1.0 / math.sqrt(length)
    for k in range(1, length // 2):
        angle = 2.0 * math.pi * (k * point % length) / length
        rows[2 * k - 1] = math.sqrt(2.0 / length) * np.cos(angle)
        rows[2 * k] = math.sqrt(2.0 / length) * np.sin(angle)
        waves[2 * k - 1] = k
        waves[2 * k] = k
    rows[length - 1] = (1.0 - 2.0 * (point % 2)) / math.sqrt(length)
    waves[length - 1] = length // 2
    order = np.argsort(waves % 2, kind="stable")
    return rows[order], waves[order]


def wave_factors(waves, length):
    freq = waves / length
    modulus = 1.0 / (2.0 / 3.0 + np.cos(2.0 * math.pi * waves / length) / 3.0) ** 2
    return freq * freq, np.exp(-((math.pi / BETA) ** 2) * freq * freq) * modulus


def halves(table):
    table = table.astype(np.float32)
    high = table.astype(ml_dtypes.bfloat16)
    low = (table - high.astype(np.float32)).astype(ml_dtypes.bfloat16)
    return high, low


def thirds(table, axis):
    table = table.astype(np.float32)
    high, middle = halves(table)
    low = (table - high.astype(np.float32)) - middle.astype(np.float32)
    return np.concatenate([low.astype(ml_dtypes.bfloat16), high, middle], axis=axis)


def finest(value, axis):
    high = value.astype(BF16)
    rest = value - high.astype(F32)
    middle = rest.astype(BF16)
    low = (rest - middle.astype(F32)).astype(BF16)
    return jnp.concatenate([high, low, middle], axis=axis)


def split(value):
    high = value.astype(BF16)
    low = (value - high.astype(F32)).astype(BF16)
    return high, low


def dot(a, b):
    return jnp.dot(a, b, preferred_element_type=F32)


def dot_nt(a, b):
    return lax.dot_general(a, b, (((1,), (1,)), ((), ())), preferred_element_type=F32)


def dot_tn(a, b):
    return lax.dot_general(a, b, (((0,), (0,)), ((), ())), preferred_element_type=F32)


def times_table(table_high, table_low, value):
    high, low = split(value)
    both = dot(table_high, jnp.concatenate([high, low], axis=1))
    return both[:, :128] + (both[:, 128:] + dot(table_low, high))


def iota(shape, dim):
    return lax.broadcasted_iota(jnp.int32, shape, dim)


def spline(u):
    d = jnp.abs(u)
    a = jnp.maximum(2.0 - d, 0.0)
    b = jnp.maximum(1.0 - d, 0.0)
    return (a * a * a - 4.0 * (b * b * b)) * (1.0 / 6.0)


def spline_slope(u):
    d = jnp.abs(u)
    a = jnp.maximum(2.0 - d, 0.0)
    b = jnp.maximum(1.0 - d, 0.0)
    slope = 0.5 * (a * a) - 2.0 * (b * b)
    return slope, (a * a * a - 4.0 * (b * b * b)) * (1.0 / 6.0)


def weights_of(u):
    slope, value = spline_slope(u)
    return value, jnp.where(u < 0.0, -slope, slope)


def prepare_kernel(
    col_in, corner_in, cell_in, fraction_in, charge_in, atoms, edge,
    col, corner, cell, fraction, charge, arrived,
):
    copies = [
        pltpu.make_async_copy(source, target, arrived.at[i])
        for i, (source, target) in enumerate(
            (
                (col_in, col), (corner_in, corner), (cell_in, cell),
                (fraction_in, fraction), (charge_in, charge),
            )
        )
    ]
    for copy in copies:
        copy.start()
    for copy in copies:
        copy.wait()
    group = iota((GROUPS, ATOMS), 0)
    hot = jnp.where((iota((GROUPS, ATOMS), 1) >> 5) == group, 1.0, 0.0).astype(BF16)
    rep_corner = dot(corner[...].astype(F32).astype(BF16), hot)
    rep_col = dot(
        jnp.broadcast_to(col[...].astype(F32), (8, GROUPS)).astype(BF16), hot
    )[0:1]
    base = rep_corner + cell[...].astype(F32)
    first = (lax.axis_index("dom") * XD).astype(F32)
    third = (lax.axis_index("pme") * ZP).astype(F32)
    along_x = (base[0:1] + first) + fraction[0:1, :]
    along_y = (base[1:2] + rep_col * float(YP)) + fraction[1:2, :]
    along_z = (base[2:3] + third) + fraction[2:3, :]
    atoms[0:1, 0:ATOMS] = along_x
    atoms[1:2, 0:ATOMS] = along_y
    atoms[2:3, 0:ATOMS] = along_z
    atoms[3:4, 0:ATOMS] = charge[...]
    atoms[:, ATOMS:] = jnp.zeros((4, 128), F32)
    lowest = (col[...] * YP + corner[1:2, :]).astype(F32)
    atoms[0:1, ATOMS : ATOMS + GROUPS] = lowest
    edge[...] = atoms[:, 0:128]


def y_starts(ya, batch, lane):
    starts = [ya[4 * batch + j] for j in range(4)]
    row = jnp.where(
        lane < 64,
        jnp.where(lane < 32, starts[0], starts[1]),
        jnp.where(lane < 96, starts[2], starts[3]),
    )
    return starts, row.astype(F32)


def masked_blocks(weights, lane):
    return jnp.concatenate(
        [jnp.where((lane >> 5) == j, weights, 0.0) for j in range(4)], axis=0
    )


def spread_batches(origin_x, origin_z, planes, ya, atoms, grid):
    lane = iota((1, 128), 1)
    step_x = iota((XW, 128), 0).astype(F32)
    step_y = iota((SPAN, 128), 0).astype(F32)
    step_z = iota((8, 128), 0).astype(F32)
    for batch in range(ATOMS // 128):
        own = slice(128 * batch, 128 * batch + 128)
        starts, base_y = y_starts(ya, batch, lane)
        xs = (atoms[0:1, own] - origin_x) + 1.0
        ys = (atoms[1:2, own] - base_y) + 1.0
        zs = (atoms[2:3, own] - origin_z) + 1.0
        wx = spline(step_x - xs)
        wz = spline(step_z - zs) * atoms[3:4, own]
        wy = masked_blocks(spline(step_y - ys), lane)
        charged = jnp.concatenate([wx * wz[z : z + 1] for z in range(planes)], axis=0)
        c_high, c_low = split(charged)
        y_high, y_low = split(wy)
        added = dot_nt(
            jnp.concatenate([y_high, y_low, y_high], axis=1),
            jnp.concatenate([c_high, c_high, c_low], axis=1),
        )
        for j in range(4):
            where = (pl.ds(starts[j], SPAN), slice(0, XW * planes))
            grid[where] = grid[where] + added[SPAN * j : SPAN * j + SPAN]


def spread_own_kernel(ya, atoms, grid):
    grid[...] = jnp.zeros((ROWS, 128), F32)
    origin_x = (lax.axis_index("dom") * XD).astype(F32)
    origin_z = (lax.axis_index("pme") * ZP).astype(F32)
    spread_batches(origin_x, origin_z, ZP, ya, atoms, grid)


def neighbour_origin():
    behind = (lax.axis_index("pme") + (N_PME - 1)) & (N_PME - 1)
    return (lax.axis_index("dom") * XD).astype(F32), (behind * ZP + ZP).astype(F32)


def spread_rest_kernel(ya, atoms, own, even_high, even_low, odd_high, odd_low, out, grid):
    grid[...] = own[...]
    origin_x, origin_z = neighbour_origin()
    spread_batches(origin_x, origin_z, ZP - 1, ya, atoms, grid)
    grid[0:16, :] = grid[0:16, :] + grid[NY:ROWS, :]
    lower = grid[0 : NY // 2, :]
    upper = grid[NY // 2 : NY, :]
    out[0 : NY // 2, :] = times_table(even_high[...], even_low[...], lower + upper)
    out[NY // 2 :, :] = times_table(odd_high[...], odd_low[...], lower - upper)


def filter_kernel(
    y_info, held, even_high, even_low, odd_high, odd_low, even_back_high, even_back_low, even_fine,
    odd_back_high, odd_back_low, odd_fine, kz_high, kz_low, tz_high, tz_low, tz_fine,
    x_square, x_factor, z_square, z_factor, out, work,
):
    lane = iota((8, 128), 1) >> 5
    for m in range(MODES):
        for a in range(8):
            blocks = [
                held[pl.ds((4 * a + b) * MODES + m, 8, stride=N_DOM * MODES), :] for b in range(4)
            ]
            for z in range(ZP):
                tile = None
                for b in range(4):
                    shift = (32 * (b - z)) % 128
                    moved = blocks[b] if shift == 0 else pltpu.roll(blocks[b], shift, 1)
                    tile = moved if tile is None else jnp.where(lane == b, moved, tile)
                row = m * NZ + z * 8
                work[row : row + 8, 128 * a : 128 * a + 128] = tile
    rows = MODES * NZ
    half = N_DOM // 2 * XW
    lower, upper = work[:, :half], work[:, half:]
    waves = []
    for value, high, low in ((lower + upper, even_high, even_low), (lower - upper, odd_high, odd_low)):
        v_high, v_low = split(value)
        both = dot(jnp.concatenate([v_high, v_low], axis=0), high[...])
        waves.append(both[:rows] + (both[rows:] + dot(v_high, low[...])))
    w_high, w_low = split(jnp.concatenate(waves, axis=1))
    full = dot(kz_high[...], w_high) + (dot(kz_high[...], w_low) + dot(kz_low[...], w_high))
    device = lax.axis_index("pme") * N_DOM + lax.axis_index("dom")
    info = y_info[pl.ds(device, 1), :]
    scaled = []
    for m in range(MODES):
        square = (x_square[...] + z_square[:, 0:1]) + info[:, m : m + 1]
        factor = (x_factor[...] * z_factor[:, 0:1]) * info[:, MODES + m : MODES + m + 1]
        nonzero = jnp.where(square > 0.0, square, 1.0)
        influence = jnp.where(square > 0.0, factor / nonzero, 0.0)
        scaled.append(full[m * NZ : m * NZ + NZ] * influence)
    scaled = jnp.concatenate(scaled, axis=0)
    s_high, s_low = split(scaled)
    back = dot(tz_high[...], s_high) + (
        dot(tz_high[...], s_low)
        + (dot(tz_low[...], s_high) + dot(tz_fine[...], finest(scaled, 0)))
    )
    parts = []
    for value, high, low, fine in (
        (back[:, : NX // 2], even_back_high, even_back_low, even_fine),
        (back[:, NX // 2 :], odd_back_high, odd_back_low, odd_fine),
    ):
        v_high, v_low = split(value)
        both = dot(jnp.concatenate([v_high, v_low], axis=0), high[...])
        small = dot(v_high, low[...]) + dot(finest(value[:, :LOW_X], 1), fine[...])
        parts.append(both[:rows] + (both[rows:] + small))
    work[:, :half] = parts[0] + parts[1]
    work[:, half:] = parts[0] - parts[1]
    for m in range(MODES):
        for a in range(8):
            tiles = [
                work[m * NZ + z * 8 : m * NZ + z * 8 + 8, 128 * a : 128 * a + 128]
                for z in range(ZP)
            ]
            for b in range(4):
                block = None
                for z in range(ZP):
                    shift = (32 * (z - b)) % 128
                    moved = tiles[z] if shift == 0 else pltpu.roll(tiles[z], shift, 1)
                    block = moved if block is None else jnp.where(lane == z, moved, block)
                out[pl.ds((4 * a + b) * MODES + m, 8, stride=N_DOM * MODES), :] = block


def gather_batches(origin_x, origin_z, planes, ya, atoms, grid, store):
    lane = iota((1, 128), 1)
    step_x = iota((XW, 128), 0).astype(F32)
    step_y = iota((SPAN, 128), 0).astype(F32)
    step_z = iota((8, 128), 0).astype(F32)
    for batch in range(ATOMS // 128):
        own = slice(128 * batch, 128 * batch + 128)
        starts, base_y = y_starts(ya, batch, lane)
        xs = (atoms[0:1, own] - origin_x) + 1.0
        ys = (atoms[1:2, own] - base_y) + 1.0
        zs = (atoms[2:3, own] - origin_z) + 1.0
        wx, sx = weights_of(step_x - xs)
        wy, sy = weights_of(step_y - ys)
        wz, sz = weights_of(step_z - zs)
        blocks = []
        level = jnp.zeros((1, 128), F32)
        for j in range(4):
            block = grid[pl.ds(starts[j], SPAN), :]
            middle = block[8:9, 44:45]
            level = jnp.where((lane >> 5) == j, middle, level)
            blocks.append((block - middle)[:, : XW * planes])
        b_high, b_low = split(jnp.concatenate(blocks, axis=0))
        y_both = jnp.concatenate([masked_blocks(wy, lane), masked_blocks(sy, lane)], axis=1)
        y_high, y_low = split(y_both)
        sampled = dot_tn(
            jnp.concatenate([b_high, b_low, b_high], axis=0),
            jnp.concatenate([y_high, y_high, y_low], axis=0),
        )
        along_x = along_y = along_z = jnp.zeros((XW, 128), F32)
        for z in range(planes):
            value = sampled[XW * z : XW * z + XW, :128]
            slope = sampled[XW * z : XW * z + XW, 128:]
            along_x = along_x + value * wz[z : z + 1]
            along_y = along_y + slope * wz[z : z + 1]
            along_z = along_z + value * sz[z : z + 1]
        minus = -atoms[3:4, own]
        kept = sz[0:1]
        for z in range(1, planes):
            kept = kept + sz[z : z + 1]
        store(
            own,
            minus * jnp.sum(along_x * sx, axis=0, keepdims=True),
            minus * jnp.sum(along_y * wx, axis=0, keepdims=True),
            minus * (jnp.sum(along_z * wx, axis=0, keepdims=True) + level * kept),
        )


def gather_rest_kernel(
    ya, atoms, held, even_high, even_low, even_fine, odd_high, odd_low, odd_fine, grid, out
):
    even = times_table(even_high[...], even_low[...], held[0 : NY // 2, :]) + dot(
        even_fine[...], finest(held[0:LOW_Y, :], 0)
    )
    odd = times_table(odd_high[...], odd_low[...], held[NY // 2 :, :]) + dot(
        odd_fine[...], finest(held[NY // 2 : NY // 2 + LOW_Y, :], 0)
    )
    grid[0 : NY // 2, :] = even + odd
    grid[NY // 2 : NY, :] = even - odd
    grid[NY:ROWS, :] = (even + odd)[0:16]
    origin_x, origin_z = neighbour_origin()

    def store(own, fx, fy, fz):
        out[0:1, own] = fx
        out[1:2, own] = fy
        out[2:3, own] = fz

    gather_batches(origin_x, origin_z, ZP - 1, ya, atoms, grid, store)


def gather_own_kernel(ya, atoms, grid, near, halo, out):
    origin_x = (lax.axis_index("dom") * XD).astype(F32)
    origin_z = (lax.axis_index("pme") * ZP).astype(F32)

    def store(own, fx, fy, fz):
        forces = [fx, fy, fz]
        for f in range(3):
            total = forces[f] + near[f : f + 1, own]
            if own.start == 0:
                total = total + halo[f : f + 1, :]
            out[f : f + 1, own] = total

    gather_batches(origin_x, origin_z, ZP, ya, atoms, grid, store)


def pair_strength(dist_sq):
    inverse = lax.rsqrt(dist_sq)
    inverse = inverse * (1.5 - 0.5 * dist_sq * inverse * inverse)
    scaled = BETA * (dist_sq * inverse)
    t = 1.0 / (1.0 + 0.5 * scaled)
    poly = jnp.full_like(t, ERFC_Q[-1])
    for coefficient in ERFC_Q[-2::-1]:
        poly = poly * t + coefficient
    fall = jnp.exp(-(BETA * BETA) * dist_sq)
    bracket = t * poly * inverse + 2.0 * BETA / math.sqrt(math.pi)
    return fall * bracket * (inverse * inverse)


def nonbonded_kernel(atoms, turned, pairs, beyond, near, halo, weight, repeated, columns):
    left = pairs[0:1, :]
    right = pairs[1:2, :]
    inside = right < CLUSTERS
    cluster = iota((CLUSTERS, PAIRS), 0)
    hot_left = jnp.where(cluster == left, 1.0, 0.0).astype(BF16)
    hot_right = jnp.where(cluster == right, 1.0, 0.0).astype(BF16)
    code = iota((16, PAIRS), 0)
    code_left = jnp.where(
        code == jnp.where(inside, right & 3, right - (CLUSTERS - 4)), 1.0, 0.0
    ).astype(BF16)
    code_right = jnp.where(
        code == jnp.where(inside, left & 3, -1), 1.0, 0.0
    ).astype(BF16)
    count = dot_nt(code_left, hot_left) + dot_nt(code_right, hot_right)
    n_high, n_low = split(count)
    expand = jnp.where(
        (iota((CLUSTERS, ATOMS), 1) >> 3) == iota((CLUSTERS, ATOMS), 0), 1.0, 0.0
    ).astype(BF16)
    weight[...] = dot(n_high, expand) + dot(n_low, expand)
    turn_1 = turned[...].astype(BF16)
    rest = turned[...] - turn_1.astype(F32)
    turn_2 = rest.astype(BF16)
    turn_3 = (rest - turn_2.astype(F32)).astype(BF16)
    spreading = jnp.where(
        (iota((GROUPS, ATOMS), 1) >> 5) == iota((GROUPS, ATOMS), 0), 1.0, 0.0
    ).astype(BF16)
    repeated[...] = (dot(turn_1, spreading) + dot(turn_2, spreading)) + dot(turn_3, spreading)
    row = iota((8, 128), 0)
    lane = iota((8, 128), 1)
    for tile in range(ATOMS // 128):
        own = slice(128 * tile, 128 * tile + 128)
        px, py, pz = atoms[0:1, own], atoms[1:2, own], atoms[2:3, own]
        sum_x = sum_y = sum_z = jnp.zeros((8, 128), F32)
        for i in range(4):
            dx = px - repeated[8 * i : 8 * i + 8, own]
            dy = py - repeated[32 + 8 * i : 40 + 8 * i, own]
            dz = pz - repeated[64 + 8 * i : 72 + 8 * i, own]
            other = repeated[96 + 8 * i : 104 + 8 * i, own]
            dist_sq = (dx * dx + dy * dy) + dz * dz
            itself = (lane & 31) == (row + 8 * i)
            dist_sq = jnp.where(itself, 1.0, dist_sq)
            strength = pair_strength(dist_sq) * (other * weight[i : i + 1, own])
            sum_x = sum_x + strength * dx
            sum_y = sum_y + strength * dy
            sum_z = sum_z + strength * dz
        near[0:1, own] = jnp.sum(sum_x, axis=0, keepdims=True)
        near[1:2, own] = jnp.sum(sum_y, axis=0, keepdims=True)
        near[2:3, own] = jnp.sum(sum_z, axis=0, keepdims=True)
    lift = jnp.where(lax.axis_index("dom") == N_DOM - 1, float(NX), 0.0)
    upright = jnp.transpose(jnp.concatenate([beyond[...]] * 32, axis=0))
    columns[...] = jnp.zeros((128, 128), F32)
    for c in range(HALO_CLUSTERS):
        part = upright[8 * c : 8 * c + 8]
        hx = part[:, 0:1] + lift
        hy = part[:, 1:2]
        hz = part[:, 2:3]
        hq = part[:, 3:4]
        sum_x = sum_y = sum_z = jnp.zeros((8, 128), F32)
        for tile in range(ATOMS // 128):
            own = slice(128 * tile, 128 * tile + 128)
            dx = atoms[0:1, own] - hx
            dy = atoms[1:2, own] - hy
            dz = atoms[2:3, own] - hz
            dist_sq = (dx * dx + dy * dy) + dz * dz
            both = weight[4 + c : 5 + c, own]
            strength = pair_strength(dist_sq) * both
            on_own = strength * hq
            near[0:1, own] = near[0:1, own] + jnp.sum(on_own * dx, axis=0, keepdims=True)
            near[1:2, own] = near[1:2, own] + jnp.sum(on_own * dy, axis=0, keepdims=True)
            near[2:3, own] = near[2:3, own] + jnp.sum(on_own * dz, axis=0, keepdims=True)
            on_halo = strength * atoms[3:4, own]
            sum_x = sum_x - on_halo * dx
            sum_y = sum_y - on_halo * dy
            sum_z = sum_z - on_halo * dz
        force_x = jnp.sum(sum_x, axis=1, keepdims=True) * hq
        force_y = jnp.sum(sum_y, axis=1, keepdims=True) * hq
        force_z = jnp.sum(sum_z, axis=1, keepdims=True) * hq
        columns[8 * c : 8 * c + 8, :] = jnp.where(
            lane == 0, force_x, jnp.where(lane == 1, force_y, jnp.where(lane == 2, force_z, 0.0))
        )
    halo[...] = jnp.transpose(columns[...])[0:8]
    for f in range(3):
        near[f : f + 1, :] = near[f : f + 1, :] * atoms[3:4, 0:ATOMS]


def call(kernel, outs, ins, scratch=(), flops=1_000_000):
    vmem = pl.BlockSpec(memory_space=pltpu.VMEM)
    smem = pl.BlockSpec(memory_space=pltpu.SMEM)
    spaces = {"s": smem, "v": vmem, "h": pl.BlockSpec(memory_space=pltpu.HBM)}
    in_specs = [spaces[kind] for kind, _ in ins]
    many = isinstance(outs, list)
    return pl.pallas_call(
        kernel,
        out_shape=outs,
        in_specs=in_specs,
        out_specs=[vmem] * len(outs) if many else vmem,
        scratch_shapes=list(scratch),
        compiler_params=pltpu.CompilerParams(vmem_limit_bytes=VMEM_LIMIT),
        cost_estimate=pl.CostEstimate(flops=flops, bytes_accessed=1_000_000, transcendentals=0),
    )(*[x for _, x in ins])


def shape(*dims):
    return jax.ShapeDtypeStruct(dims, F32)


def permuted(x, axis, by):
    length = lax.axis_size(axis)
    return lax.ppermute(x, axis, [(i, (i + by) % length) for i in range(length)])


def exchange(x):
    sent = x.reshape(DEVICES, 1, MODES * 128)
    return lax.all_to_all(sent, ("pme", "dom"), 0, 0).reshape(DEVICES * MODES, 128)


def tables():
    along_y, y_waves = real_basis(NY)
    along_x, x_waves = real_basis(NX)
    along_z, z_waves = real_basis(NZ)
    folded = np.zeros((N_DOM * XW, NX))
    for q in range(N_DOM):
        for x in range(XD + 3):
            folded[q * XW + x] = along_x[:, (q * XD + x) % NX]
    order = np.array([4 * p + z for z in range(ZP) for p in range(N_PME)])
    z_rows = np.kron(np.eye(MODES), along_z[:, order])
    y_square, y_factor = wave_factors(y_waves, NY)
    y_info = np.zeros((DEVICES, 128))
    y_info[:, 0:MODES] = y_square.reshape(DEVICES, MODES)
    y_info[:, MODES : 2 * MODES] = y_factor.reshape(DEVICES, MODES)
    x_square, x_factor = wave_factors(x_waves, NX)
    z_square, z_factor = wave_factors(z_waves, NZ)
    f32 = np.float32
    even = folded[: N_DOM // 2 * XW, : NX // 2]
    odd = folded[: N_DOM // 2 * XW, NX // 2 :]

    def back(table, low):
        return (*halves(table), thirds(table[:, :low], 1))

    return {
        "y_even": halves(along_y[: NY // 2, : NY // 2]),
        "y_odd": halves(along_y[NY // 2 :, : NY // 2]),
        "y_even_back": back(along_y[: NY // 2, : NY // 2].T, LOW_Y),
        "y_odd_back": back(along_y[NY // 2 :, : NY // 2].T, LOW_Y),
        "x_even": halves(even),
        "x_odd": halves(odd),
        "x_even_back": (*halves(even.T), thirds(even.T[:LOW_X], 0)),
        "x_odd_back": (*halves(odd.T), thirds(odd.T[:LOW_X], 0)),
        "z": halves(z_rows),
        "z_back": back(z_rows.T, MODES * NZ),
        "y_info": y_info.astype(f32),
        "x_square": x_square.astype(f32)[None, :],
        "x_factor": (x_factor / math.pi).astype(f32)[None, :],
        "z_square": np.repeat(z_square.astype(f32)[:, None], 128, axis=1),
        "z_factor": np.repeat(z_factor.astype(f32)[:, None], 128, axis=1),
    }


def make_shards(table):
    def shards(group_column, group_corner, atom_cell, fraction, charge, cluster_pairs):
        column = group_column.reshape(1, GROUPS)
        atoms, edge = call(
            prepare_kernel,
            [shape(4, CARRIED), shape(4, 128)],
            [
                ("h", pltpu.with_memory_space_constraint(column, pltpu.HBM)),
                ("h", pltpu.with_memory_space_constraint(group_corner, pltpu.HBM)),
                ("h", pltpu.with_memory_space_constraint(atom_cell, pltpu.HBM)),
                ("h", pltpu.with_memory_space_constraint(fraction, pltpu.HBM)),
                ("h", pltpu.with_memory_space_constraint(charge.reshape(1, ATOMS), pltpu.HBM)),
            ],
            scratch=[
                pltpu.VMEM((1, GROUPS), jnp.int32),
                pltpu.VMEM((3, GROUPS), jnp.int32),
                pltpu.VMEM((3, ATOMS), jnp.int32),
                pltpu.VMEM((3, ATOMS), F32),
                pltpu.VMEM((1, ATOMS), F32),
                pltpu.SemaphoreType.DMA((5,)),
            ],
        )
        behind = permuted(atoms, "pme", 1)
        beyond = permuted(edge, "dom", -1)
        ya = column[0] * YP + group_corner[1]
        own_grid = call(
            spread_own_kernel,
            shape(ROWS, 128),
            [("s", ya), ("v", atoms)],
            flops=3_000_000_000,
        )
        ya_behind = behind[0, ATOMS : ATOMS + GROUPS].astype(jnp.int32)
        spectrum = call(
            spread_rest_kernel,
            shape(NY, 128),
            [
                ("s", ya_behind), ("v", behind), ("v", own_grid),
                *[("v", x) for x in table["y_even"] + table["y_odd"]],
            ],
            scratch=[pltpu.VMEM((ROWS, 128), F32)],
        )
        held = exchange(spectrum)
        turned = atoms[:, :ATOMS].reshape(4, GROUPS, 32).transpose(0, 2, 1).reshape(128, GROUPS)
        near, halo = call(
            nonbonded_kernel,
            [shape(3, ATOMS), shape(8, 128)],
            [("v", atoms), ("v", turned), ("v", cluster_pairs), ("v", beyond)],
            scratch=[
                pltpu.VMEM((16, ATOMS), F32),
                pltpu.VMEM((128, ATOMS), F32),
                pltpu.VMEM((128, 128), F32),
            ],
            flops=8_000_000_000,
        )
        halo_back = permuted(halo, "dom", 1)
        filtered = call(
            filter_kernel,
            shape(DEVICES * MODES, 128),
            [
                ("v", table["y_info"]), ("v", held),
                *[("v", x) for x in table["x_even"] + table["x_odd"]],
                *[("v", x) for x in table["x_even_back"] + table["x_odd_back"]],
                *[("v", x) for x in table["z"] + table["z_back"]],
                ("v", table["x_square"]), ("v", table["x_factor"]),
                ("v", table["z_square"]), ("v", table["z_factor"]),
            ],
            scratch=[pltpu.VMEM((MODES * NZ, N_DOM * XW), F32)],
        )
        returned = exchange(filtered)
        grid, rest = call(
            gather_rest_kernel,
            [shape(ROWS, 128), shape(3, ATOMS)],
            [
                ("s", ya_behind), ("v", behind), ("v", returned),
                *[("v", x) for x in table["y_even_back"] + table["y_odd_back"]],
            ],
        )
        rest_back = permuted(rest, "pme", -1)
        forces = call(
            gather_own_kernel,
            shape(3, ATOMS),
            [
                ("s", ya), ("v", atoms), ("v", grid), ("v", near),
                ("v", halo_back),
            ],
            flops=3_000_000_000,
        )
        return forces + rest_back

    return shards


def solution(mesh):
    in_specs = (
        P(("pme", "dom"), None),
        P(None, ("pme", "dom")),
        P(None, ("pme", "dom")),
        P(None, ("pme", "dom")),
        P(("pme", "dom")),
        P(None, ("pme", "dom")),
    )
    out_specs = P(None, ("pme", "dom"))
    return jax.shard_map(
        make_shards(tables()), mesh=mesh, in_specs=in_specs, out_specs=out_specs, check_vma=False
    )
```

```python
import math

import jax
import jax.numpy as jnp
import ml_dtypes
import numpy as np
from jax import lax
from jax.experimental import pallas as pl
from jax.experimental.pallas import tpu as pltpu
from jax.sharding import PartitionSpec as P

NX = 768
NY = 768
NZ = 32
N_DOM = 32
N_PME = 8
DEVICES = 256
XD = 24
YP = 24
ZP = 4
GROUPS = 64
ATOMS = 2048
CARRIED = ATOMS + 128
PAIRS = 1024
CLUSTERS = 256
HALO_CLUSTERS = 8
HALO_ATOMS = 64
XW = 32
MODES = 3
LOW_Y = 64
LOW_X = 128
ROWS = NY + 16
SPAN = 16
BETA = 0.35
VMEM_LIMIT = 24 * 1024 * 1024

F32 = jnp.float32
BF16 = jnp.bfloat16

ERFC_Q = (
    0.2820947951,
    0.2820937768,
    0.2468838798,
    0.1753240754,
    0.0934147485,
    -0.05905091002,
    0.1318500403,
    -0.4545637183,
    0.493385742,
    -0.2346054907,
    0.04317306594,
)


def real_basis(length):
    point = np.arange(length)
    rows = np.zeros((length, length))
    waves = np.zeros(length, np.int64)
    rows[0] = 1.0 / math.sqrt(length)
    for k in range(1, length // 2):
        angle = 2.0 * math.pi * (k * point % length) / length
        rows[2 * k - 1] = math.sqrt(2.0 / length) * np.cos(angle)
        rows[2 * k] = math.sqrt(2.0 / length) * np.sin(angle)
        waves[2 * k - 1] = k
        waves[2 * k] = k
    rows[length - 1] = (1.0 - 2.0 * (point % 2)) / math.sqrt(length)
    waves[length - 1] = length // 2
    order = np.argsort(waves % 2, kind="stable")
    return rows[order], waves[order]


def wave_factors(waves, length):
    freq = waves / length
    modulus = 1.0 / (2.0 / 3.0 + np.cos(2.0 * math.pi * waves / length) / 3.0) ** 2
    return freq * freq, np.exp(-((math.pi / BETA) ** 2) * freq * freq) * modulus


def halves(table):
    table = table.astype(np.float32)
    high = table.astype(ml_dtypes.bfloat16)
    low = (table - high.astype(np.float32)).astype(ml_dtypes.bfloat16)
    return high, low


def thirds(table, axis):
    table = table.astype(np.float32)
    high, middle = halves(table)
    low = (table - high.astype(np.float32)) - middle.astype(np.float32)
    return np.concatenate([low.astype(ml_dtypes.bfloat16), high, middle], axis=axis)


def finest(value, axis):
    high = value.astype(BF16)
    rest = value - high.astype(F32)
    middle = rest.astype(BF16)
    low = (rest - middle.astype(F32)).astype(BF16)
    return jnp.concatenate([high, low, middle], axis=axis)


def split(value):
    high = value.astype(BF16)
    low = (value - high.astype(F32)).astype(BF16)
    return high, low


def dot(a, b):
    return jnp.dot(a, b, preferred_element_type=F32)


def dot_nt(a, b):
    return lax.dot_general(a, b, (((1,), (1,)), ((), ())), preferred_element_type=F32)


def dot_tn(a, b):
    return lax.dot_general(a, b, (((0,), (0,)), ((), ())), preferred_element_type=F32)


def times_table(table_high, table_low, value):
    high, low = split(value)
    both = dot(table_high, jnp.concatenate([high, low], axis=1))
    return both[:, :128] + (both[:, 128:] + dot(table_low, high))


def iota(shape, dim):
    return lax.broadcasted_iota(jnp.int32, shape, dim)


def spline(u):
    d = jnp.abs(u)
    a = jnp.maximum(2.0 - d, 0.0)
    b = jnp.maximum(1.0 - d, 0.0)
    return (a * a * a - 4.0 * (b * b * b)) * (1.0 / 6.0)


def spline_slope(u):
    d = jnp.abs(u)
    a = jnp.maximum(2.0 - d, 0.0)
    b = jnp.maximum(1.0 - d, 0.0)
    slope = 0.5 * (a * a) - 2.0 * (b * b)
    return slope, (a * a * a - 4.0 * (b * b * b)) * (1.0 / 6.0)


def weights_of(u):
    slope, value = spline_slope(u)
    return value, jnp.where(u < 0.0, -slope, slope)


def prepare_kernel(
    col_in, corner_in, cell_in, fraction_in, charge_in, atoms, edge,
    col, corner, cell, fraction, charge, arrived,
):
    copies = [
        pltpu.make_async_copy(source, target, arrived.at[i])
        for i, (source, target) in enumerate(
            (
                (col_in, col), (corner_in, corner), (cell_in, cell),
                (fraction_in, fraction), (charge_in, charge),
            )
        )
    ]
    for copy in copies:
        copy.start()
    for copy in copies:
        copy.wait()
    group = iota((GROUPS, ATOMS), 0)
    hot = jnp.where((iota((GROUPS, ATOMS), 1) >> 5) == group, 1.0, 0.0).astype(BF16)
    rep_corner = dot(corner[...].astype(F32).astype(BF16), hot)
    rep_col = dot(
        jnp.broadcast_to(col[...].astype(F32), (8, GROUPS)).astype(BF16), hot
    )[0:1]
    base = rep_corner + cell[...].astype(F32)
    first = (lax.axis_index("dom") * XD).astype(F32)
    third = (lax.axis_index("pme") * ZP).astype(F32)
    along_x = (base[0:1] + first) + fraction[0:1, :]
    along_y = (base[1:2] + rep_col * float(YP)) + fraction[1:2, :]
    along_z = (base[2:3] + third) + fraction[2:3, :]
    atoms[0:1, 0:ATOMS] = along_x
    atoms[1:2, 0:ATOMS] = along_y
    atoms[2:3, 0:ATOMS] = along_z
    atoms[3:4, 0:ATOMS] = charge[...]
    atoms[:, ATOMS:] = jnp.zeros((4, 128), F32)
    lowest = (col[...] * YP + corner[1:2, :]).astype(F32)
    atoms[0:1, ATOMS : ATOMS + GROUPS] = lowest
    edge[...] = atoms[:, 0:128]


def y_starts(ya, batch, lane):
    starts = [ya[4 * batch + j] for j in range(4)]
    row = jnp.where(
        lane < 64,
        jnp.where(lane < 32, starts[0], starts[1]),
        jnp.where(lane < 96, starts[2], starts[3]),
    )
    return starts, row.astype(F32)


def masked_blocks(weights, lane):
    return jnp.concatenate(
        [jnp.where((lane >> 5) == j, weights, 0.0) for j in range(4)], axis=0
    )


def spread_batches(origin_x, origin_z, planes, ya, atoms, grid):
    lane = iota((1, 128), 1)
    step_x = iota((XW, 128), 0).astype(F32)
    step_y = iota((SPAN, 128), 0).astype(F32)
    step_z = iota((8, 128), 0).astype(F32)
    for batch in range(ATOMS // 128):
        own = slice(128 * batch, 128 * batch + 128)
        starts, base_y = y_starts(ya, batch, lane)
        xs = (atoms[0:1, own] - origin_x) + 1.0
        ys = (atoms[1:2, own] - base_y) + 1.0
        zs = (atoms[2:3, own] - origin_z) + 1.0
        wx = spline(step_x - xs)
        wz = spline(step_z - zs) * atoms[3:4, own]
        wy = masked_blocks(spline(step_y - ys), lane)
        charged = jnp.concatenate([wx * wz[z : z + 1] for z in range(planes)], axis=0)
        c_high, c_low = split(charged)
        y_high, y_low = split(wy)
        added = dot_nt(
            jnp.concatenate([y_high, y_low, y_high], axis=1),
            jnp.concatenate([c_high, c_high, c_low], axis=1),
        )
        for j in range(4):
            where = (pl.ds(starts[j], SPAN), slice(0, XW * planes))
            grid[where] = grid[where] + added[SPAN * j : SPAN * j + SPAN]


def spread_own_kernel(ya, atoms, grid):
    grid[...] = jnp.zeros((ROWS, 128), F32)
    origin_x = (lax.axis_index("dom") * XD).astype(F32)
    origin_z = (lax.axis_index("pme") * ZP).astype(F32)
    spread_batches(origin_x, origin_z, ZP, ya, atoms, grid)


def neighbour_origin():
    behind = (lax.axis_index("pme") + (N_PME - 1)) & (N_PME - 1)
    return (lax.axis_index("dom") * XD).astype(F32), (behind * ZP + ZP).astype(F32)


def spread_rest_kernel(ya, atoms, own, even_high, even_low, odd_high, odd_low, out, grid):
    grid[...] = own[...]
    origin_x, origin_z = neighbour_origin()
    spread_batches(origin_x, origin_z, ZP - 1, ya, atoms, grid)
    grid[0:16, :] = grid[0:16, :] + grid[NY:ROWS, :]
    lower = grid[0 : NY // 2, :]
    upper = grid[NY // 2 : NY, :]
    out[0 : NY // 2, :] = times_table(even_high[...], even_low[...], lower + upper)
    out[NY // 2 :, :] = times_table(odd_high[...], odd_low[...], lower - upper)


def filter_kernel(
    y_info, held, even_high, even_low, odd_high, odd_low, even_back_high, even_back_low, even_fine,
    odd_back_high, odd_back_low, odd_fine, kz, tz,
    x_square, x_factor, z_square, z_factor, out, work,
):
    lane = iota((8, 128), 1) >> 5
    for m in range(MODES):
        for a in range(8):
            blocks = [
                held[pl.ds((4 * a + b) * MODES + m, 8, stride=N_DOM * MODES), :] for b in range(4)
            ]
            for z in range(ZP):
                tile = None
                for b in range(4):
                    shift = (32 * (b - z)) % 128
                    moved = blocks[b] if shift == 0 else pltpu.roll(blocks[b], shift, 1)
                    tile = moved if tile is None else jnp.where(lane == b, moved, tile)
                row = m * NZ + z * 8
                work[row : row + 8, 128 * a : 128 * a + 128] = tile
    rows = MODES * NZ
    half = N_DOM // 2 * XW
    lower, upper = work[:, :half], work[:, half:]
    waves = []
    for value, high, low in ((lower + upper, even_high, even_low), (lower - upper, odd_high, odd_low)):
        v_high, v_low = split(value)
        both = dot(jnp.concatenate([v_high, v_low], axis=0), high[...])
        waves.append(both[:rows] + (both[rows:] + dot(v_high, low[...])))
    w_high, w_low = split(jnp.concatenate(waves, axis=1))
    full = dot(kz[...], jnp.concatenate([w_high, w_low, w_high], axis=0))
    device = lax.axis_index("pme") * N_DOM + lax.axis_index("dom")
    info = y_info[pl.ds(device, 1), :]
    scaled = []
    for m in range(MODES):
        square = (x_square[...] + z_square[:, 0:1]) + info[:, m : m + 1]
        factor = (x_factor[...] * z_factor[:, 0:1]) * info[:, MODES + m : MODES + m + 1]
        nonzero = jnp.where(square > 0.0, square, 1.0)
        influence = jnp.where(square > 0.0, factor / nonzero, 0.0)
        scaled.append(full[m * NZ : m * NZ + NZ] * influence)
    scaled = jnp.concatenate(scaled, axis=0)
    s_high, s_low = split(scaled)
    back = dot(
        tz[...], jnp.concatenate([s_high, s_low, s_high, finest(scaled, 0)], axis=0)
    )
    parts = []
    for value, high, low, fine in (
        (back[:, : NX // 2], even_back_high, even_back_low, even_fine),
        (back[:, NX // 2 :], odd_back_high, odd_back_low, odd_fine),
    ):
        v_high, v_low = split(value)
        both = dot(jnp.concatenate([v_high, v_low], axis=0), high[...])
        small = dot(v_high, low[...]) + dot(finest(value[:, :LOW_X], 1), fine[...])
        parts.append(both[:rows] + (both[rows:] + small))
    work[:, :half] = parts[0] + parts[1]
    work[:, half:] = parts[0] - parts[1]
    for m in range(MODES):
        for a in range(8):
            tiles = [
                work[m * NZ + z * 8 : m * NZ + z * 8 + 8, 128 * a : 128 * a + 128]
                for z in range(ZP)
            ]
            for b in range(4):
                block = None
                for z in range(ZP):
                    shift = (32 * (z - b)) % 128
                    moved = tiles[z] if shift == 0 else pltpu.roll(tiles[z], shift, 1)
                    block = moved if block is None else jnp.where(lane == z, moved, block)
                out[pl.ds((4 * a + b) * MODES + m, 8, stride=N_DOM * MODES), :] = block


def gather_batches(origin_x, origin_z, planes, ya, atoms, grid, store):
    lane = iota((1, 128), 1)
    step_x = iota((XW, 128), 0).astype(F32)
    step_y = iota((SPAN, 128), 0).astype(F32)
    step_z = iota((8, 128), 0).astype(F32)
    for batch in range(ATOMS // 128):
        own = slice(128 * batch, 128 * batch + 128)
        starts, base_y = y_starts(ya, batch, lane)
        xs = (atoms[0:1, own] - origin_x) + 1.0
        ys = (atoms[1:2, own] - base_y) + 1.0
        zs = (atoms[2:3, own] - origin_z) + 1.0
        wx, sx = weights_of(step_x - xs)
        wy, sy = weights_of(step_y - ys)
        wz, sz = weights_of(step_z - zs)
        blocks = []
        level = jnp.zeros((1, 128), F32)
        for j in range(4):
            block = grid[pl.ds(starts[j], SPAN), :]
            middle = block[8:9, 44:45]
            level = jnp.where((lane >> 5) == j, middle, level)
            blocks.append((block - middle)[:, : XW * planes])
        b_high, b_low = split(jnp.concatenate(blocks, axis=0))
        y_both = jnp.concatenate([masked_blocks(wy, lane), masked_blocks(sy, lane)], axis=1)
        y_high, y_low = split(y_both)
        sampled = dot_tn(
            jnp.concatenate([b_high, b_low, b_high], axis=0),
            jnp.concatenate([y_high, y_high, y_low], axis=0),
        )
        along_x = along_y = along_z = jnp.zeros((XW, 128), F32)
        for z in range(planes):
            value = sampled[XW * z : XW * z + XW, :128]
            slope = sampled[XW * z : XW * z + XW, 128:]
            along_x = along_x + value * wz[z : z + 1]
            along_y = along_y + slope * wz[z : z + 1]
            along_z = along_z + value * sz[z : z + 1]
        minus = -atoms[3:4, own]
        kept = sz[0:1]
        for z in range(1, planes):
            kept = kept + sz[z : z + 1]
        store(
            own,
            minus * jnp.sum(along_x * sx, axis=0, keepdims=True),
            minus * jnp.sum(along_y * wx, axis=0, keepdims=True),
            minus * (jnp.sum(along_z * wx, axis=0, keepdims=True) + level * kept),
        )


def gather_rest_kernel(
    ya, atoms, held, even_high, even_low, even_fine, odd_high, odd_low, odd_fine, grid, out
):
    even = times_table(even_high[...], even_low[...], held[0 : NY // 2, :]) + dot(
        even_fine[...], finest(held[0:LOW_Y, :], 0)
    )
    odd = times_table(odd_high[...], odd_low[...], held[NY // 2 :, :]) + dot(
        odd_fine[...], finest(held[NY // 2 : NY // 2 + LOW_Y, :], 0)
    )
    grid[0 : NY // 2, :] = even + odd
    grid[NY // 2 : NY, :] = even - odd
    grid[NY:ROWS, :] = (even + odd)[0:16]
    origin_x, origin_z = neighbour_origin()

    def store(own, fx, fy, fz):
        out[0:1, own] = fx
        out[1:2, own] = fy
        out[2:3, own] = fz

    gather_batches(origin_x, origin_z, ZP - 1, ya, atoms, grid, store)


def gather_own_kernel(ya, atoms, grid, near, halo, out):
    origin_x = (lax.axis_index("dom") * XD).astype(F32)
    origin_z = (lax.axis_index("pme") * ZP).astype(F32)

    def store(own, fx, fy, fz):
        forces = [fx, fy, fz]
        for f in range(3):
            total = forces[f] + near[f : f + 1, own]
            if own.start == 0:
                total = total + halo[f : f + 1, :]
            out[f : f + 1, own] = total

    gather_batches(origin_x, origin_z, ZP, ya, atoms, grid, store)


def pair_strength(dist_sq):
    inverse = lax.rsqrt(dist_sq)
    inverse = inverse * (1.5 - 0.5 * dist_sq * inverse * inverse)
    scaled = BETA * (dist_sq * inverse)
    t = 1.0 / (1.0 + 0.5 * scaled)
    poly = jnp.full_like(t, ERFC_Q[-1])
    for coefficient in ERFC_Q[-2::-1]:
        poly = poly * t + coefficient
    fall = jnp.exp(-(BETA * BETA) * dist_sq)
    bracket = t * poly * inverse + 2.0 * BETA / math.sqrt(math.pi)
    return fall * bracket * (inverse * inverse)


def nonbonded_kernel(atoms, turned, pairs, beyond, near, halo, weight, repeated, columns):
    left = pairs[0:1, :]
    right = pairs[1:2, :]
    inside = right < CLUSTERS
    cluster = iota((CLUSTERS, PAIRS), 0)
    hot_left = jnp.where(cluster == left, 1.0, 0.0).astype(BF16)
    hot_right = jnp.where(cluster == right, 1.0, 0.0).astype(BF16)
    code = iota((16, PAIRS), 0)
    code_left = jnp.where(
        code == jnp.where(inside, right & 3, right - (CLUSTERS - 4)), 1.0, 0.0
    ).astype(BF16)
    code_right = jnp.where(
        code == jnp.where(inside, left & 3, -1), 1.0, 0.0
    ).astype(BF16)
    count = dot_nt(code_left, hot_left) + dot_nt(code_right, hot_right)
    n_high, n_low = split(count)
    expand = jnp.where(
        (iota((CLUSTERS, ATOMS), 1) >> 3) == iota((CLUSTERS, ATOMS), 0), 1.0, 0.0
    ).astype(BF16)
    weight[...] = dot(n_high, expand) + dot(n_low, expand)
    turn_1 = turned[...].astype(BF16)
    rest = turned[...] - turn_1.astype(F32)
    turn_2 = rest.astype(BF16)
    turn_3 = (rest - turn_2.astype(F32)).astype(BF16)
    spreading = jnp.where(
        (iota((GROUPS, ATOMS), 1) >> 5) == iota((GROUPS, ATOMS), 0), 1.0, 0.0
    ).astype(BF16)
    repeated[...] = (dot(turn_1, spreading) + dot(turn_2, spreading)) + dot(turn_3, spreading)
    row = iota((8, 128), 0)
    lane = iota((8, 128), 1)
    for tile in range(ATOMS // 128):
        own = slice(128 * tile, 128 * tile + 128)
        px, py, pz = atoms[0:1, own], atoms[1:2, own], atoms[2:3, own]
        sum_x = sum_y = sum_z = jnp.zeros((8, 128), F32)
        for i in range(4):
            dx = px - repeated[8 * i : 8 * i + 8, own]
            dy = py - repeated[32 + 8 * i : 40 + 8 * i, own]
            dz = pz - repeated[64 + 8 * i : 72 + 8 * i, own]
            other = repeated[96 + 8 * i : 104 + 8 * i, own]
            dist_sq = (dx * dx + dy * dy) + dz * dz
            itself = (lane & 31) == (row + 8 * i)
            dist_sq = jnp.where(itself, 1.0, dist_sq)
            strength = pair_strength(dist_sq) * (other * weight[i : i + 1, own])
            sum_x = sum_x + strength * dx
            sum_y = sum_y + strength * dy
            sum_z = sum_z + strength * dz
        near[0:1, own] = jnp.sum(sum_x, axis=0, keepdims=True)
        near[1:2, own] = jnp.sum(sum_y, axis=0, keepdims=True)
        near[2:3, own] = jnp.sum(sum_z, axis=0, keepdims=True)
    lift = jnp.where(lax.axis_index("dom") == N_DOM - 1, float(NX), 0.0)
    upright = jnp.transpose(jnp.concatenate([beyond[...]] * 32, axis=0))
    columns[...] = jnp.zeros((128, 128), F32)
    for c in range(HALO_CLUSTERS):
        part = upright[8 * c : 8 * c + 8]
        hx = part[:, 0:1] + lift
        hy = part[:, 1:2]
        hz = part[:, 2:3]
        hq = part[:, 3:4]
        sum_x = sum_y = sum_z = jnp.zeros((8, 128), F32)
        for tile in range(ATOMS // 128):
            own = slice(128 * tile, 128 * tile + 128)
            dx = atoms[0:1, own] - hx
            dy = atoms[1:2, own] - hy
            dz = atoms[2:3, own] - hz
            dist_sq = (dx * dx + dy * dy) + dz * dz
            both = weight[4 + c : 5 + c, own]
            strength = pair_strength(dist_sq) * both
            on_own = strength * hq
            near[0:1, own] = near[0:1, own] + jnp.sum(on_own * dx, axis=0, keepdims=True)
            near[1:2, own] = near[1:2, own] + jnp.sum(on_own * dy, axis=0, keepdims=True)
            near[2:3, own] = near[2:3, own] + jnp.sum(on_own * dz, axis=0, keepdims=True)
            on_halo = strength * atoms[3:4, own]
            sum_x = sum_x - on_halo * dx
            sum_y = sum_y - on_halo * dy
            sum_z = sum_z - on_halo * dz
        force_x = jnp.sum(sum_x, axis=1, keepdims=True) * hq
        force_y = jnp.sum(sum_y, axis=1, keepdims=True) * hq
        force_z = jnp.sum(sum_z, axis=1, keepdims=True) * hq
        columns[8 * c : 8 * c + 8, :] = jnp.where(
            lane == 0, force_x, jnp.where(lane == 1, force_y, jnp.where(lane == 2, force_z, 0.0))
        )
    halo[...] = jnp.transpose(columns[...])[0:8]
    for f in range(3):
        near[f : f + 1, :] = near[f : f + 1, :] * atoms[3:4, 0:ATOMS]


def call(kernel, outs, ins, scratch=(), flops=1_000_000):
    vmem = pl.BlockSpec(memory_space=pltpu.VMEM)
    smem = pl.BlockSpec(memory_space=pltpu.SMEM)
    spaces = {"s": smem, "v": vmem, "h": pl.BlockSpec(memory_space=pltpu.HBM)}
    in_specs = [spaces[kind] for kind, _ in ins]
    many = isinstance(outs, list)
    return pl.pallas_call(
        kernel,
        out_shape=outs,
        in_specs=in_specs,
        out_specs=[vmem] * len(outs) if many else vmem,
        scratch_shapes=list(scratch),
        compiler_params=pltpu.CompilerParams(vmem_limit_bytes=VMEM_LIMIT),
        cost_estimate=pl.CostEstimate(flops=flops, bytes_accessed=1_000_000, transcendentals=0),
    )(*[x for _, x in ins])


def shape(*dims):
    return jax.ShapeDtypeStruct(dims, F32)


def permuted(x, axis, by):
    length = lax.axis_size(axis)
    return lax.ppermute(x, axis, [(i, (i + by) % length) for i in range(length)])


def exchange(x):
    sent = x.reshape(DEVICES, 1, MODES * 128)
    return lax.all_to_all(sent, ("pme", "dom"), 0, 0).reshape(DEVICES * MODES, 128)


def tables():
    along_y, y_waves = real_basis(NY)
    along_x, x_waves = real_basis(NX)
    along_z, z_waves = real_basis(NZ)
    folded = np.zeros((N_DOM * XW, NX))
    for q in range(N_DOM):
        for x in range(XD + 3):
            folded[q * XW + x] = along_x[:, (q * XD + x) % NX]
    order = np.array([4 * p + z for z in range(ZP) for p in range(N_PME)])
    z_rows = np.kron(np.eye(MODES), along_z[:, order])
    y_square, y_factor = wave_factors(y_waves, NY)
    y_info = np.zeros((DEVICES, 128))
    y_info[:, 0:MODES] = y_square.reshape(DEVICES, MODES)
    y_info[:, MODES : 2 * MODES] = y_factor.reshape(DEVICES, MODES)
    x_square, x_factor = wave_factors(x_waves, NX)
    z_square, z_factor = wave_factors(z_waves, NZ)
    f32 = np.float32
    even = folded[: N_DOM // 2 * XW, : NX // 2]
    odd = folded[: N_DOM // 2 * XW, NX // 2 :]

    def along(table):
        high, low = halves(table)
        return np.concatenate([high, high, low], axis=1)

    def back(table, low):
        return (*halves(table), thirds(table[:, :low], 1))

    return {
        "y_even": halves(along_y[: NY // 2, : NY // 2]),
        "y_odd": halves(along_y[NY // 2 :, : NY // 2]),
        "y_even_back": back(along_y[: NY // 2, : NY // 2].T, LOW_Y),
        "y_odd_back": back(along_y[NY // 2 :, : NY // 2].T, LOW_Y),
        "x_even": halves(even),
        "x_odd": halves(odd),
        "x_even_back": (*halves(even.T), thirds(even.T[:LOW_X], 0)),
        "x_odd_back": (*halves(odd.T), thirds(odd.T[:LOW_X], 0)),
        "z": along(z_rows),
        "z_back": np.concatenate([along(z_rows.T), thirds(z_rows.T, 1)], axis=1),
        "y_info": y_info.astype(f32),
        "x_square": x_square.astype(f32)[None, :],
        "x_factor": (x_factor / math.pi).astype(f32)[None, :],
        "z_square": np.repeat(z_square.astype(f32)[:, None], 128, axis=1),
        "z_factor": np.repeat(z_factor.astype(f32)[:, None], 128, axis=1),
    }


def make_shards(table):
    def shards(group_column, group_corner, atom_cell, fraction, charge, cluster_pairs):
        column = group_column.reshape(1, GROUPS)
        atoms, edge = call(
            prepare_kernel,
            [shape(4, CARRIED), shape(4, 128)],
            [
                ("h", pltpu.with_memory_space_constraint(column, pltpu.HBM)),
                ("h", pltpu.with_memory_space_constraint(group_corner, pltpu.HBM)),
                ("h", pltpu.with_memory_space_constraint(atom_cell, pltpu.HBM)),
                ("h", pltpu.with_memory_space_constraint(fraction, pltpu.HBM)),
                ("h", pltpu.with_memory_space_constraint(charge.reshape(1, ATOMS), pltpu.HBM)),
            ],
            scratch=[
                pltpu.VMEM((1, GROUPS), jnp.int32),
                pltpu.VMEM((3, GROUPS), jnp.int32),
                pltpu.VMEM((3, ATOMS), jnp.int32),
                pltpu.VMEM((3, ATOMS), F32),
                pltpu.VMEM((1, ATOMS), F32),
                pltpu.SemaphoreType.DMA((5,)),
            ],
        )
        behind = permuted(atoms, "pme", 1)
        beyond = permuted(edge, "dom", -1)
        ya = column[0] * YP + group_corner[1]
        own_grid = call(
            spread_own_kernel,
            shape(ROWS, 128),
            [("s", ya), ("v", atoms)],
            flops=3_000_000_000,
        )
        ya_behind = behind[0, ATOMS : ATOMS + GROUPS].astype(jnp.int32)
        spectrum = call(
            spread_rest_kernel,
            shape(NY, 128),
            [
                ("s", ya_behind), ("v", behind), ("v", own_grid),
                *[("v", x) for x in table["y_even"] + table["y_odd"]],
            ],
            scratch=[pltpu.VMEM((ROWS, 128), F32)],
        )
        held = exchange(spectrum)
        turned = atoms[:, :ATOMS].reshape(4, GROUPS, 32).transpose(0, 2, 1).reshape(128, GROUPS)
        near, halo = call(
            nonbonded_kernel,
            [shape(3, ATOMS), shape(8, 128)],
            [("v", atoms), ("v", turned), ("v", cluster_pairs), ("v", beyond)],
            scratch=[
                pltpu.VMEM((16, ATOMS), F32),
                pltpu.VMEM((128, ATOMS), F32),
                pltpu.VMEM((128, 128), F32),
            ],
            flops=8_000_000_000,
        )
        halo_back = permuted(halo, "dom", 1)
        filtered = call(
            filter_kernel,
            shape(DEVICES * MODES, 128),
            [
                ("v", table["y_info"]), ("v", held),
                *[("v", x) for x in table["x_even"] + table["x_odd"]],
                *[("v", x) for x in table["x_even_back"] + table["x_odd_back"]],
                ("v", table["z"]), ("v", table["z_back"]),
                ("v", table["x_square"]), ("v", table["x_factor"]),
                ("v", table["z_square"]), ("v", table["z_factor"]),
            ],
            scratch=[pltpu.VMEM((MODES * NZ, N_DOM * XW), F32)],
        )
        returned = exchange(filtered)
        grid, rest = call(
            gather_rest_kernel,
            [shape(ROWS, 128), shape(3, ATOMS)],
            [
                ("s", ya_behind), ("v", behind), ("v", returned),
                *[("v", x) for x in table["y_even_back"] + table["y_odd_back"]],
            ],
        )
        rest_back = permuted(rest, "pme", -1)
        forces = call(
            gather_own_kernel,
            shape(3, ATOMS),
            [
                ("s", ya), ("v", atoms), ("v", grid), ("v", near),
                ("v", halo_back),
            ],
            flops=3_000_000_000,
        )
        return forces + rest_back

    return shards


def solution(mesh):
    in_specs = (
        P(("pme", "dom"), None),
        P(None, ("pme", "dom")),
        P(None, ("pme", "dom")),
        P(None, ("pme", "dom")),
        P(("pme", "dom")),
        P(None, ("pme", "dom")),
    )
    out_specs = P(None, ("pme", "dom"))
    return jax.shard_map(
        make_shards(tables()), mesh=mesh, in_specs=in_specs, out_specs=out_specs, check_vma=False
    )
```
